512 devices in a mesh: band: 8 (over y_lo, x), dom: 64 (over z, y_hi, core).
Axes of the slice: x: 4, y: 8 (y_hi: 4, y_lo: 2; y = y_hi * 2 + y_lo), z: 8, core: 2. Of those that a mesh axis runs over, the one named last changes fastest.
Arguments:
- orbitals: float32 [256, 384, 256], P('band', 'dom'), may hold values from -6 to 6
- potential: float32 [384, 256], P('dom'), may hold values from -1 to 0.5
Outputs:
- orthonormal: float32 [256, 384, 256], P('band', 'dom')
The draws below stay inside these ranges and needn't reach their ends.
All inputs are finite; a program needn't handle non-finite values.
Results may differ from the reference program's by a relative error of at most 0.00007.
Values sent between devices are 32-bit elements; how exact they have to be, the bound alone decides.
A program may use at most 64 MiB of HBM per device.

```python
import jax
import jax.numpy as jnp
from jax import lax

ORB = 32
NX = 16
NY = 16
BANDS = 256
NZ = 384
CELLS = 98304
N_BAND = 8


def block_scale(rng, shape, shards, low, largest):
    def one(axis_at, parts):
        draws = jax.random.uniform(jax.random.fold_in(jax.random.fold_in(rng, 6), axis_at), (parts,), jnp.float32, low / len(shards), largest / len(shards))
        return jnp.repeat(jnp.exp(draws), shape[axis_at] // parts).reshape((-1,) + (1,) * (len(shape) - axis_at - 1))

    level = one(*shards[0])
    for cut in shards[1:]:
        level = level * one(*cut)
    return level


def bell_draw(key, shape, deviation, bound, cuts=(), kind=jnp.bfloat16):
    values = jax.random.normal(key, shape, jnp.float32) * deviation
    if len(cuts) > 0:
        values = block_scale(key, shape, cuts, -0.22, 0.18) * values
    return jnp.clip(values, min=-bound, max=bound).astype(kind)


def setup_inputs(seed: int = 0) -> dict:
    key_of = jax.random.split(jax.random.key(seed), 3)
    orbitals = bell_draw(key_of[0], (BANDS, NZ, NY * NX), 1.0, 6.0, ((0, 8), (1, 64)), jnp.float32)
    potential = jnp.clip(-1.0 + 1.5 * jax.random.uniform(key_of[1], (NZ, NY * NX), jnp.float32) ** block_scale(key_of[1], (NZ, NY * NX), ((0, 64),), -0.2, 0.2), -1.0, 0.5)
    return dict(orbitals=orbitals, potential=potential)


weights = (-5369.0 / 1800.0, 12.0 / 7.0, -15.0 / 56.0, 10.0 / 189.0, -1.0 / 112.0, 2.0 / 1925.0, -1.0 / 16632.0)
centre = 6.0
half_width = 5.0

def hamiltonian(field, potential):
    bands = field.shape[0]
    lap = 3.0 * weights[0] * field
    for step in range(1, 7):
        lap = lap + weights[step] * (jnp.roll(field, step, 1) + jnp.roll(field, -step, 1))
    grid = field.reshape(bands, field.shape[1], NY, NX)
    side = jnp.zeros_like(grid)
    for step in range(1, 7):
        side = side + weights[step] * (jnp.roll(grid, step, 2) + jnp.roll(grid, -step, 2) + jnp.roll(grid, step, 3) + jnp.roll(grid, -step, 3))
    lap = lap + side.reshape(field.shape)
    return -0.5 * lap + potential[None] * field

def filter_block(block, potential):

    def scaled(field):
        return (hamiltonian(field, potential) - centre * field) / half_width
    first = scaled(block)
    second = 2.0 * scaled(first) - block
    return 2.0 * scaled(second) - first

def reference(orbitals, potential):
    groups = orbitals.reshape(N_BAND, ORB, NZ, NY * NX)
    filtered = lax.map(lambda block: filter_block(block, potential), groups)
    flat = filtered.reshape(BANDS, NZ * NY * NX)
    margin = jnp.dot(flat.astype(jnp.float32), flat.T.astype(jnp.float32), precision=lax.Precision.HIGHEST, preferred_element_type=jnp.float32) / jnp.float32(CELLS)
    factor = jnp.linalg.cholesky(margin)
    inverse = lax.linalg.triangular_solve(factor, jnp.eye(BANDS, dtype=margin.dtype), left_side=True, lower=True)
    result = jnp.dot(inverse.astype(jnp.float32), flat.astype(jnp.float32), precision=lax.Precision.HIGHEST, preferred_element_type=jnp.float32)
    return result.reshape(BANDS, NZ, NY * NX)
```

```python
import jax
import jax.numpy as jnp
import numpy as np
from jax import lax
from jax.experimental import pallas as pl
from jax.experimental.pallas import tpu as pltpu
from jax.sharding import PartitionSpec as P

NX = 16
ORB = 32
BANDS = 256
PLANES = 6
WIDTH = 256
CELLS = 98304
GROUPS = 8
CHUNKS = 4
CORB = ORB // CHUNKS
PIVOTS = 4
HALF = BANDS // 2

weights = (
    -5369.0 / 1800.0,
    12.0 / 7.0,
    -15.0 / 56.0,
    10.0 / 189.0,
    -1.0 / 112.0,
    2.0 / 1925.0,
    -1.0 / 16632.0,
)
centre = 6.0
half_width = 5.0
along_z = [-0.5 * w / half_width for w in weights]

FAR_BAND = (2, 6, 3, 5, 1, 7, 4)
FAR_HI = (2, 1, 3)
FAR_Z = (4, 3, 5, 2, 6, 1, 7)
MESH = pl.DeviceIdType.MESH
EXACT = lax.Precision.HIGHEST
F32 = jnp.float32


def plane_matrix():
    out = np.zeros((WIDTH, WIDTH))
    for cell in range(WIDTH):
        y, x = divmod(cell, NX)
        out[cell, cell] += 3.0 * weights[0]
        for step in range(1, 7):
            for sign in (-1, 1):
                out[(y + sign * step) % NX * NX + x, cell] += weights[step]
                out[y * NX + (x + sign * step) % NX, cell] += weights[step]
    return (-0.5 / half_width * out).astype(np.float32)


def product(a, b, dims=((1,), (0,))):
    return lax.dot_general(
        a, b, (dims, ((), ())), precision=EXACT, preferred_element_type=F32
    )


def greet(partners):
    barrier = pltpu.get_barrier_semaphore()
    for partner in partners:
        pl.semaphore_signal(barrier, inc=1, device_id=partner, device_id_type=MESH)
    pl.semaphore_wait(barrier, len(partners))


def send(src, dst, send_sem, recv_sem, device):
    copy = pltpu.make_async_remote_copy(
        src_ref=src,
        dst_ref=dst,
        send_sem=send_sem,
        recv_sem=recv_sem,
        device_id=device,
        device_id_type=MESH,
    )
    return copy


def eliminate(groups, size):
    lane = lax.broadcasted_iota(jnp.int32, (8, size), 1)
    sublane = lax.broadcasted_iota(jnp.int32, (8, size), 0)
    groups = list(groups)
    span = range(PIVOTS)

    def spread_lane(tile, at):
        return jnp.broadcast_to(tile[:, at:at + 1], (8, size))

    def spread_row(tile, at):
        return jnp.broadcast_to(tile[at:at + 1, :], (8, size))

    entry = None
    for first in range(0, size, PIVOTS):
        home, off = divmod(first, 8)
        live = range(home, size // 8)
        columns = [{g: spread_lane(groups[g], first + q) for g in live} for q in span]
        if entry is None:
            entry = [[spread_row(columns[q][home], off + p) for q in range(p + 1)] for p in span]
        following = first + PIVOTS
        if following < size:
            near, near_off = divmod(following, 8)
            ahead = [spread_lane(groups[near], following + q) for q in span]
            ahead = [[spread_row(ahead[q], near_off + p) for q in range(p + 1)] for p in span]
            coupling = [[spread_row(columns[t][near], near_off + p) for t in span] for p in span]
        inside = (lane >= first) & (lane < following)
        scales = []
        low = [[None] * PIVOTS for _ in span]
        for q in span:
            value = entry[q][q]
            for t in range(q):
                value = value - low[q][t] * low[q][t]
            scales.append(lax.rsqrt(value))
            for p in range(q + 1, PIVOTS):
                value = entry[p][q]
                for t in range(q):
                    value = value - low[p][t] * low[q][t]
                low[p][q] = value * scales[q]
        if following < size:
            for t in span:
                for p in span:
                    value = coupling[p][t]
                    for u in range(t):
                        value = value - low[t][u] * coupling[p][u]
                    coupling[p][t] = value * scales[t]
            for p in span:
                for q in range(p + 1):
                    value = ahead[p][q]
                    for t in span:
                        value = value - coupling[p][t] * coupling[q][t]
                    ahead[p][q] = value
            entry = ahead
        scaled = []
        pivot_rows = []
        for q in span:
            column = dict(columns[q])
            row = spread_row(groups[home], off + q)
            row = jnp.where(inside, jnp.where(lane == first + q, 1.0, 0.0), row)
            for t in range(q):
                row = row - low[q][t] * pivot_rows[t]
                for g in live:
                    column[g] = column[g] - low[q][t] * scaled[t][g]
            pivot_rows.append(row * scales[q])
            scaled.append({g: column[g] * scales[q] for g in live})
        for g in live:
            if g == home and following % 8 == 0:
                new = groups[g]
            else:
                new = jnp.where(inside, 0.0, groups[g])
                for q in span:
                    new = new - scaled[q][g] * pivot_rows[q]
                if g == home:
                    new = jnp.where(sublane < off, groups[g], new)
            if g == home:
                for q in span:
                    new = jnp.where(sublane == off + q, pivot_rows[q], new)
            groups[g] = new
    return groups


def rows_of(b):
    return pl.ds(pl.multiple_of(b * ORB, ORB), ORB)


def whole_kernel(x_ref, pot_hbm, mat_hbm, out_ref, pot_ref, mat_ref, cells_ref, margin_ref, made, work,
                 field, local, part, band_in, hi_in, z_in,
                 halo_send, halo_recv, cell_sems, load_sems, sems, row_sems):
    band = lax.axis_index("band")
    dom = lax.axis_index("dom")
    count = lax.axis_size("dom")
    core = lax.rem(dom, 2)
    hi = lax.rem(lax.div(dom, 2), 4)
    z = lax.div(dom, 8)
    left = (band, lax.rem(dom + count - 1, count))
    right = (band, lax.rem(dom + 1, count))
    bands = [lax.rem(band + k, 8) for k in range(8)]
    senders = [lax.rem(band + 8 - k, 8) for k in range(8)]
    to_band = [(bands[k], dom) for k in range(8)]
    to_hi = [(band, z * 8 + lax.rem(hi + k, 4) * 2 + core) for k in range(4)]
    to_z = [(band, lax.rem(z + k, 8) * 8 + hi * 2 + core) for k in range(8)]
    has_plane = band < PLANES
    loads = [
        pltpu.make_async_copy(x_ref, field.at[0, pl.ds(PLANES, PLANES)], load_sems.at[0]),
        pltpu.make_async_copy(mat_hbm, mat_ref, load_sems.at[1]),
        pltpu.make_async_copy(pot_hbm, pot_ref, load_sems.at[2]),
    ]
    for load in loads:
        load.start()
    to_sixteen = [
        (k, flip, (bands[k], dom + flip * (1 - 2 * core)))
        for k in FAR_BAND + (0,) for flip in range(2) if k + flip > 0
    ]
    own = core * 8 + band
    greet([left, right] + [where for _, _, where in to_sixteen] + to_hi[1:] + to_z[1:])

    def chunk(c):
        return pl.ds(c * CORB, CORB)

    def halo(r, c):
        if r == 0:
            own = x_ref.at[:, chunk(c)]
        else:
            own = field.at[r, pl.ds(PLANES, PLANES), chunk(c)]
        return (
            send(own, field.at[r, pl.ds(2 * PLANES, PLANES), chunk(c)],
                 halo_send.at[r, c, 0], halo_recv.at[r, c, 0], left),
            send(own, field.at[r, pl.ds(0, PLANES), chunk(c)],
                 halo_send.at[r, c, 1], halo_recv.at[r, c, 1], right),
        )

    def in_plane(r, c):
        own = field[r, PLANES:2 * PLANES, c * CORB:(c + 1) * CORB, :]
        flat = own.reshape(PLANES * CORB, WIDTH)
        side = product(flat, mat_ref[...]).reshape(PLANES, CORB, WIDTH)
        for p in range(PLANES):
            diag = (pot_ref[p:p + 1, :] - centre) * (1.0 / half_width)
            local[c, p] = side[p] + diag * own[p]

    def rows_in(c):
        return pl.ds(pl.multiple_of(band * ORB, ORB) + c * CORB, CORB)

    def to_plane(k, c):
        return send(field.at[3, PLANES + bands[k], chunk(c)], cells_ref.at[rows_in(c)],
                    cell_sems.at[0], cell_sems.at[1], to_band[k])

    def all_planes():
        others = cells_ref.at[pl.ds(0, BANDS - ORB)]
        return send(others, others, cell_sems.at[0], cell_sems.at[1], to_band[1])

    for c in range(CHUNKS):
        for copy in halo(0, c):
            copy.start()
    for load in loads:
        load.wait()
    for c in range(CHUNKS):
        in_plane(0, c)
    for r in range(3):
        for c in range(CHUNKS):
            rows = slice(c * CORB, (c + 1) * CORB)
            for copy in halo(r, c):
                copy.wait_recv()
            for p in range(PLANES):
                total = local[c, p]
                for step in range(1, 7):
                    total = total + along_z[step] * (
                        field[r, PLANES + p - step, rows, :] + field[r, PLANES + p + step, rows, :]
                    )
                if r > 0:
                    total = 2.0 * total - field[r - 1, PLANES + p, rows, :]
                field[r + 1, PLANES + p, rows, :] = total
            if r < 2:
                for copy in halo(r + 1, c):
                    copy.start()
                in_plane(r + 1, c)
            else:
                for k in FAR_BAND:
                    @pl.when(bands[k] < PLANES)
                    def _():
                        to_plane(k, c).start()

                @pl.when(has_plane)
                def _():
                    cells_ref[rows_in(c), :] = field[3, PLANES + band, rows, :]

    def sixteenth(k, flip):
        return (core + flip * (1 - 2 * core)) * 8 + bands[k]

    parts = (pl.ds(0, 8), pl.ds(8, 16))

    def total_of(ref, count, i):
        total = ref[0, parts[i], :]
        for t in range(1, count):
            total = total + ref[t, parts[i], :]
        return total

    def bytes_of(ref, count, stage, i):
        some = ref.at[pl.ds(0, count), parts[i]]
        return send(some, some, sems.at[stage, 0, i], sems.at[stage, 1, i], left)

    def to_owner(k, flip, where, i):
        return send(part.at[sixteenth(k, flip), parts[i]], band_in.at[core * PLANES + band, parts[i]],
                    sems.at[0, 0, i], sems.at[0, 1, i], where)

    @pl.when(has_plane)
    def _():
        all_planes().wait_recv()
        for i in range(2):
            if i == 0:
                blocks = (product(cells_ref[:HALF, :], cells_ref[:HALF, :], ((1,), (1,))),)
            else:
                both = product(cells_ref[HALF:, :], cells_ref[...], ((1,), (1,)))
                blocks = (both[:, :HALF], both[:, HALF:])
            for q in range(16):
                for n, piece in enumerate(blocks):
                    part[q, 8 * (i + n):8 * (i + n) + 8, :] = piece[8 * q:8 * q + 8, :]
            for target in to_sixteen:
                to_owner(*target, i).start()
            band_in[core * PLANES + band, parts[i], :] = part[own, parts[i], :]

    def across_hi(k, i):
        mine = hi_in.at[hi, parts[i]]
        return send(mine, mine, sems.at[1, 0, i], sems.at[1, 1, i], to_hi[k])

    for i in range(2):
        @pl.when(has_plane)
        def _():
            bytes_of(band_in, 11, 0, i).wait_recv()

        @pl.when(jnp.logical_not(has_plane))
        def _():
            bytes_of(band_in, 12, 0, i).wait_recv()

        hi_in[hi, parts[i], :] = total_of(band_in, 12, i)
        for k in FAR_HI:
            across_hi(k, i).start()

    for c in range(CHUNKS):
        for r in range(3):
            for copy in halo(r, c):
                copy.wait_send()

    def across_z(k, i):
        mine = z_in.at[z, parts[i]]
        return send(mine, mine, sems.at[2, 0, i], sems.at[2, 1, i], to_z[k])

    for i in range(2):
        bytes_of(hi_in, 3, 1, i).wait_recv()
        z_in[z, parts[i], :] = total_of(hi_in, 4, i)
        for k in FAR_Z:
            across_z(k, i).start()

    def sent_planes(count):
        out = field.at[3, pl.ds(PLANES, count)]
        return send(out, out, cell_sems.at[0], cell_sems.at[1], left)

    @pl.when(jnp.logical_not(has_plane))
    def _():
        sent_planes(PLANES).wait_send()

    @pl.when(has_plane)
    def _():
        sent_planes(PLANES - 1).wait_send()
        for i in range(2):
            bytes_of(part, 15, 0, i).wait_send()

    def gather(where, i):
        mine = margin_ref.at[own, parts[i]]
        return send(mine, mine, sems.at[3, 0, i], sems.at[3, 1, i], where)

    for i in range(2):
        bytes_of(hi_in, 3, 1, i).wait_send()
        bytes_of(z_in, 7, 2, i).wait_recv()
        margin_ref[own, parts[i], :] = total_of(z_in, 8, i) * F32(1.0 / CELLS)
        for k, flip, where in to_sixteen:
            @pl.when(bands[k] < PLANES)
            def _():
                gather(where, i).start()

    def to_rows(half, k):
        target = half * 4 + lax.rem(band + k, 4)
        return send(made.at[rows_of(target)], out_ref.at[band],
                    row_sems.at[0, half * 4 + k], row_sems.at[1, band], (target, dom))

    def from_plane(p):
        return send(made.at[rows_of(0)], out_ref.at[p],
                    row_sems.at[0, 0], row_sems.at[1, p], (p, dom))

    lane = lax.broadcasted_iota(jnp.int32, (HALF, HALF), 1)
    row = lax.broadcasted_iota(jnp.int32, (HALF, HALF), 0)

    def block(i):
        return jnp.concatenate([margin_ref[q, 8 * i:8 * i + 8, :] for q in range(16)], axis=0)

    def factor_of(at):
        done = eliminate([work[at, 8 * g:8 * g + 8, :] for g in range(HALF // 8)], HALF)
        for g in range(HALF // 8):
            work[at, 8 * g:8 * g + 8, :] = done[g]
        return jnp.where(row >= lane, work[at], 0.0)

    def hand_out(half):
        for k in range(4):
            if k == 0:
                @pl.when(lax.div(band, 4) != half)
                def _():
                    to_rows(half, k).start()

                @pl.when(lax.div(band, 4) == half)
                def _():
                    out_ref[band] = made[rows_of(band), :]
            else:
                to_rows(half, k).start()

    @pl.when(jnp.logical_not(has_plane))
    def _():
        for i in range(2):
            bytes_of(z_in, 7, 2, i).wait_send()
            bytes_of(margin_ref, 12, 3, i).wait_send()

    @pl.when(has_plane)
    def _():
        bytes_of(margin_ref, 15, 3, 0).wait_recv()
        work[0] = block(0)
        first = factor_of(0)
        bytes_of(margin_ref, 15, 3, 1).wait_recv()
        below = product(block(1), first, ((1,), (1,)))
        work[1] = block(2) - product(below, below, ((1,), (1,)))
        made[:HALF, :] = product(first, cells_ref[:HALF, :])
        hand_out(0)
        for i in range(2):
            bytes_of(z_in, 7, 2, i).wait_send()
            bytes_of(margin_ref, 11, 3, i).wait_send()
        made[HALF:, :] = cells_ref[HALF:, :] - product(below, made[:HALF, :])
        second = factor_of(1)
        made[HALF:, :] = product(second, made[HALF:, :])
        hand_out(1)

    for p in range(PLANES):
        @pl.when(band != p)
        def _():
            from_plane(p).wait_recv()

    @pl.when(has_plane)
    def _():
        for half in range(2):
            for k in range(4):
                if k == 0:
                    @pl.when(lax.div(band, 4) != half)
                    def _():
                        to_rows(half, k).wait_send()
                else:
                    to_rows(half, k).wait_send()


def on_device(orbitals, potential):
    dma = pltpu.SemaphoreType.DMA
    piece = (24, 128)
    in_vmem = pl.BlockSpec(memory_space=pltpu.VMEM)
    planes = pl.pallas_call(
        whole_kernel,
        out_shape=pltpu.VMEM((PLANES, ORB, WIDTH), F32),
        in_specs=[pl.BlockSpec(memory_space=pltpu.HBM)] * 3,
        out_specs=in_vmem,
        scratch_shapes=[
            pltpu.VMEM((PLANES, WIDTH), F32),
            pltpu.VMEM((WIDTH, WIDTH), F32),
            pltpu.VMEM((BANDS, WIDTH), F32),
            pltpu.VMEM((16,) + piece, F32),
            pltpu.VMEM((BANDS, WIDTH), F32),
            pltpu.VMEM((2, HALF, HALF), F32),
            pltpu.VMEM((4, 3 * PLANES, ORB, WIDTH), F32),
            pltpu.VMEM((CHUNKS, PLANES, CORB, WIDTH), F32),
            pltpu.VMEM((16,) + piece, F32),
            pltpu.VMEM((2 * PLANES,) + piece, F32),
            pltpu.VMEM((4,) + piece, F32),
            pltpu.VMEM((8,) + piece, F32),
            dma((3, CHUNKS, 2)),
            dma((3, CHUNKS, 2)),
            dma((2,)),
            dma((3,)),
            dma((4, 2, 2)),
            dma((2, 8)),
        ],
        compiler_params=pltpu.CompilerParams(
            collective_id=0, has_side_effects=True, vmem_limit_bytes=54 * 1024 * 1024
        ),
        name="filter_orthonormalize",
    )(jnp.transpose(orbitals, (1, 0, 2)), potential, jnp.asarray(plane_matrix()))
    return jnp.transpose(planes, (1, 0, 2))


def solution(mesh):
    placed = (P("band", "dom", None), P("dom", None))
    return jax.shard_map(
        on_device, mesh=mesh, in_specs=placed, out_specs=P("band", "dom", None), check_vma=False
    )
```

```python
import jax
import jax.numpy as jnp
import numpy as np
from jax import lax
from jax.experimental import pallas as pl
from jax.experimental.pallas import tpu as pltpu
from jax.sharding import PartitionSpec as P

NX = 16
ORB = 32
BANDS = 256
PLANES = 6
WIDTH = 256
CELLS = 98304
GROUPS = 8
CHUNKS = 4
CORB = ORB // CHUNKS
PIVOTS = 4
HALF = BANDS // 2

weights = (
    -5369.0 / 1800.0,
    12.0 / 7.0,
    -15.0 / 56.0,
    10.0 / 189.0,
    -1.0 / 112.0,
    2.0 / 1925.0,
    -1.0 / 16632.0,
)
centre = 6.0
half_width = 5.0
along_z = [-0.5 * w / half_width for w in weights]

FAR_BAND = (2, 6, 3, 5, 1, 7, 4)
FAR_HI = (2, 1, 3)
FAR_Z = (4, 3, 5, 2, 6, 1, 7)
MESH = pl.DeviceIdType.MESH
EXACT = lax.Precision.HIGHEST
F32 = jnp.float32


def plane_matrix():
    out = np.zeros((WIDTH, WIDTH))
    for cell in range(WIDTH):
        y, x = divmod(cell, NX)
        out[cell, cell] += 3.0 * weights[0]
        for step in range(1, 7):
            for sign in (-1, 1):
                out[(y + sign * step) % NX * NX + x, cell] += weights[step]
                out[y * NX + (x + sign * step) % NX, cell] += weights[step]
    return (-0.5 / half_width * out).astype(np.float32)


def product(a, b, dims=((1,), (0,))):
    return lax.dot_general(
        a, b, (dims, ((), ())), precision=EXACT, preferred_element_type=F32
    )


def greet(partners):
    barrier = pltpu.get_barrier_semaphore()
    for partner in partners:
        pl.semaphore_signal(barrier, inc=1, device_id=partner, device_id_type=MESH)
    pl.semaphore_wait(barrier, len(partners))


def send(src, dst, send_sem, recv_sem, device):
    copy = pltpu.make_async_remote_copy(
        src_ref=src,
        dst_ref=dst,
        send_sem=send_sem,
        recv_sem=recv_sem,
        device_id=device,
        device_id_type=MESH,
    )
    return copy


def eliminate(groups, size, after_block=None):
    lane = lax.broadcasted_iota(jnp.int32, (8, size), 1)
    sublane = lax.broadcasted_iota(jnp.int32, (8, size), 0)
    groups = list(groups)
    span = range(PIVOTS)

    def spread_lane(tile, at):
        return jnp.broadcast_to(tile[:, at:at + 1], (8, size))

    def spread_row(tile, at):
        return jnp.broadcast_to(tile[at:at + 1, :], (8, size))

    entry = None
    for first in range(0, size, PIVOTS):
        home, off = divmod(first, 8)
        live = range(home, size // 8)
        columns = [{g: spread_lane(groups[g], first + q) for g in live} for q in span]
        if entry is None:
            entry = [[spread_row(columns[q][home], off + p) for q in range(p + 1)] for p in span]
        following = first + PIVOTS
        if following < size:
            near, near_off = divmod(following, 8)
            ahead = [spread_lane(groups[near], following + q) for q in span]
            ahead = [[spread_row(ahead[q], near_off + p) for q in range(p + 1)] for p in span]
            coupling = [[spread_row(columns[t][near], near_off + p) for t in span] for p in span]
        inside = (lane >= first) & (lane < following)
        scales = []
        low = [[None] * PIVOTS for _ in span]
        for q in span:
            value = entry[q][q]
            for t in range(q):
                value = value - low[q][t] * low[q][t]
            scales.append(lax.rsqrt(value))
            for p in range(q + 1, PIVOTS):
                value = entry[p][q]
                for t in range(q):
                    value = value - low[p][t] * low[q][t]
                low[p][q] = value * scales[q]
        if following < size:
            for t in span:
                for p in span:
                    value = coupling[p][t]
                    for u in range(t):
                        value = value - low[t][u] * coupling[p][u]
                    coupling[p][t] = value * scales[t]
            for p in span:
                for q in range(p + 1):
                    value = ahead[p][q]
                    for t in span:
                        value = value - coupling[p][t] * coupling[q][t]
                    ahead[p][q] = value
            entry = ahead
        scaled = []
        pivot_rows = []
        for q in span:
            column = dict(columns[q])
            row = spread_row(groups[home], off + q)
            row = jnp.where(inside, jnp.where(lane == first + q, 1.0, 0.0), row)
            for t in range(q):
                row = row - low[q][t] * pivot_rows[t]
                for g in live:
                    column[g] = column[g] - low[q][t] * scaled[t][g]
            pivot_rows.append(row * scales[q])
            scaled.append({g: column[g] * scales[q] for g in live})
        for g in live:
            if g == home and following % 8 == 0:
                new = groups[g]
            else:
                new = jnp.where(inside, 0.0, groups[g])
                for q in span:
                    new = new - scaled[q][g] * pivot_rows[q]
                if g == home:
                    new = jnp.where(sublane < off, groups[g], new)
            if g == home:
                for q in span:
                    new = jnp.where(sublane == off + q, pivot_rows[q], new)
            groups[g] = new
        if after_block is not None and following % ORB == 0:
            after_block(following // ORB - 1, groups)
    return groups


def rows_of(b):
    return pl.ds(pl.multiple_of(b * ORB, ORB), ORB)


def whole_kernel(x_ref, pot_hbm, mat_hbm, out_ref, pot_ref, mat_ref, cells_ref, margin_ref, made, work, below_ref,
                 field, local, part, band_in, hi_in, z_in,
                 halo_send, halo_recv, cell_sems, load_sems, sems, row_sems):
    band = lax.axis_index("band")
    dom = lax.axis_index("dom")
    count = lax.axis_size("dom")
    core = lax.rem(dom, 2)
    hi = lax.rem(lax.div(dom, 2), 4)
    z = lax.div(dom, 8)
    left = (band, lax.rem(dom + count - 1, count))
    right = (band, lax.rem(dom + 1, count))
    bands = [lax.rem(band + k, 8) for k in range(8)]
    senders = [lax.rem(band + 8 - k, 8) for k in range(8)]
    to_band = [(bands[k], dom) for k in range(8)]
    to_hi = [(band, z * 8 + lax.rem(hi + k, 4) * 2 + core) for k in range(4)]
    to_z = [(band, lax.rem(z + k, 8) * 8 + hi * 2 + core) for k in range(8)]
    has_plane = band < PLANES
    loads = [
        pltpu.make_async_copy(x_ref, field.at[0, pl.ds(PLANES, PLANES)], load_sems.at[0]),
        pltpu.make_async_copy(mat_hbm, mat_ref, load_sems.at[1]),
        pltpu.make_async_copy(pot_hbm, pot_ref, load_sems.at[2]),
    ]
    for load in loads:
        load.start()
    to_sixteen = [
        (k, flip, (bands[k], dom + flip * (1 - 2 * core)))
        for k in FAR_BAND + (0,) for flip in range(2) if k + flip > 0
    ]
    own = core * 8 + band
    greet([to_z[k] for k in FAR_Z] + [to_hi[k] for k in FAR_HI] + [left, right]
          + [where for _, _, where in to_sixteen])

    def chunk(c):
        return pl.ds(c * CORB, CORB)

    def halo(r, c):
        if r == 0:
            own = x_ref.at[:, chunk(c)]
        else:
            own = field.at[r, pl.ds(PLANES, PLANES), chunk(c)]
        return (
            send(own, field.at[r, pl.ds(2 * PLANES, PLANES), chunk(c)],
                 halo_send.at[r, c, 0], halo_recv.at[r, c, 0], left),
            send(own, field.at[r, pl.ds(0, PLANES), chunk(c)],
                 halo_send.at[r, c, 1], halo_recv.at[r, c, 1], right),
        )

    def in_plane(r, c):
        own = field[r, PLANES:2 * PLANES, c * CORB:(c + 1) * CORB, :]
        flat = own.reshape(PLANES * CORB, WIDTH)
        side = product(flat, mat_ref[...]).reshape(PLANES, CORB, WIDTH)
        for p in range(PLANES):
            diag = (pot_ref[p:p + 1, :] - centre) * (1.0 / half_width)
            local[c, p] = side[p] + diag * own[p]

    def rows_in(c):
        return pl.ds(pl.multiple_of(band * ORB, ORB) + c * CORB, CORB)

    def to_plane(k, c):
        return send(field.at[3, PLANES + bands[k], chunk(c)], cells_ref.at[rows_in(c)],
                    cell_sems.at[0], cell_sems.at[1], to_band[k])

    def all_planes():
        others = cells_ref.at[pl.ds(0, BANDS - ORB)]
        return send(others, others, cell_sems.at[0], cell_sems.at[1], to_band[1])

    for c in range(CHUNKS):
        for copy in halo(0, c):
            copy.start()
    for load in loads:
        load.wait()
    for c in range(CHUNKS):
        in_plane(0, c)
    for r in range(3):
        for c in range(CHUNKS):
            rows = slice(c * CORB, (c + 1) * CORB)
            for copy in halo(r, c):
                copy.wait_recv()
            for p in range(PLANES):
                total = local[c, p]
                for step in range(1, 7):
                    total = total + along_z[step] * (
                        field[r, PLANES + p - step, rows, :] + field[r, PLANES + p + step, rows, :]
                    )
                if r > 0:
                    total = 2.0 * total - field[r - 1, PLANES + p, rows, :]
                field[r + 1, PLANES + p, rows, :] = total
            if r < 2:
                for copy in halo(r + 1, c):
                    copy.start()
                in_plane(r + 1, c)
            else:
                for k in FAR_BAND:
                    @pl.when(bands[k] < PLANES)
                    def _():
                        to_plane(k, c).start()

                @pl.when(has_plane)
                def _():
                    cells_ref[rows_in(c), :] = field[3, PLANES + band, rows, :]

    def sixteenth(k, flip):
        return (core + flip * (1 - 2 * core)) * 8 + bands[k]

    parts = (pl.ds(0, 8), pl.ds(8, 16))

    def total_of(ref, count, i):
        total = ref[0, parts[i], :]
        for t in range(1, count):
            total = total + ref[t, parts[i], :]
        return total

    def bytes_of(ref, count, stage, i):
        some = ref.at[pl.ds(0, count), parts[i]]
        return send(some, some, sems.at[stage, 0, i], sems.at[stage, 1, i], left)

    def to_owner(k, flip, where, i):
        return send(part.at[sixteenth(k, flip), parts[i]], band_in.at[core * PLANES + band, parts[i]],
                    sems.at[0, 0, i], sems.at[0, 1, i], where)

    @pl.when(has_plane)
    def _():
        all_planes().wait_recv()
        for i in range(2):
            if i == 0:
                blocks = (product(cells_ref[:HALF, :], cells_ref[:HALF, :], ((1,), (1,))),)
            else:
                both = product(cells_ref[HALF:, :], cells_ref[...], ((1,), (1,)))
                blocks = (both[:, :HALF], both[:, HALF:])
            for q in range(16):
                for n, piece in enumerate(blocks):
                    part[q, 8 * (i + n):8 * (i + n) + 8, :] = piece[8 * q:8 * q + 8, :]
            for target in to_sixteen:
                to_owner(*target, i).start()
            band_in[core * PLANES + band, parts[i], :] = part[own, parts[i], :]

    def across_hi(k, i):
        mine = hi_in.at[hi, parts[i]]
        return send(mine, mine, sems.at[1, 0, i], sems.at[1, 1, i], to_hi[k])

    for i in range(2):
        @pl.when(has_plane)
        def _():
            bytes_of(band_in, 11, 0, i).wait_recv()

        @pl.when(jnp.logical_not(has_plane))
        def _():
            bytes_of(band_in, 12, 0, i).wait_recv()

        hi_in[hi, parts[i], :] = total_of(band_in, 12, i)
        for k in FAR_HI:
            across_hi(k, i).start()

    for c in range(CHUNKS):
        for r in range(3):
            for copy in halo(r, c):
                copy.wait_send()

    def across_z(k, i):
        mine = z_in.at[z, parts[i]]
        return send(mine, mine, sems.at[2, 0, i], sems.at[2, 1, i], to_z[k])

    for i in range(2):
        bytes_of(hi_in, 3, 1, i).wait_recv()
        z_in[z, parts[i], :] = total_of(hi_in, 4, i)
        for k in FAR_Z:
            across_z(k, i).start()

    def sent_planes(count):
        out = field.at[3, pl.ds(PLANES, count)]
        return send(out, out, cell_sems.at[0], cell_sems.at[1], left)

    @pl.when(jnp.logical_not(has_plane))
    def _():
        sent_planes(PLANES).wait_send()

    @pl.when(has_plane)
    def _():
        sent_planes(PLANES - 1).wait_send()
        for i in range(2):
            bytes_of(part, 15, 0, i).wait_send()

    def gather(where, i):
        mine = margin_ref.at[own, parts[i]]
        return send(mine, mine, sems.at[3, 0, i], sems.at[3, 1, i], where)

    for i in range(2):
        bytes_of(hi_in, 3, 1, i).wait_send()
        bytes_of(z_in, 7, 2, i).wait_recv()
        margin_ref[own, parts[i], :] = total_of(z_in, 8, i) * F32(1.0 / CELLS)
        for k, flip, where in to_sixteen:
            @pl.when(bands[k] < PLANES)
            def _():
                gather(where, i).start()

    def to_rows(t):
        return send(made.at[pl.ds(t * ORB, ORB)], out_ref.at[band],
                    row_sems.at[0, t], row_sems.at[1, band], (t, dom))

    def from_plane(p):
        return send(made.at[rows_of(0)], out_ref.at[p],
                    row_sems.at[0, 0], row_sems.at[1, p], (p, dom))

    lane = lax.broadcasted_iota(jnp.int32, (HALF, HALF), 1)
    row = lax.broadcasted_iota(jnp.int32, (HALF, HALF), 0)

    def block(i):
        return jnp.concatenate([margin_ref[q, 8 * i:8 * i + 8, :] for q in range(16)], axis=0)

    def groups_of(at):
        return [work[at, 8 * g:8 * g + 8, :] for g in range(HALF // 8)]

    def hand_out(t):
        @pl.when(band != t)
        def _():
            to_rows(t).start()

        @pl.when(band == t)
        def _():
            out_ref[t] = made[t * ORB:(t + 1) * ORB, :]

    def multiply(groups, begin, end):
        rows = jnp.concatenate(groups[begin // 8:end // 8], axis=0)
        rows = jnp.where(row[begin:end] >= lane[begin:end], rows, 0.0)
        made[HALF + begin:HALF + end, :] = product(rows, cells_ref[HALF:, :])

    def after_block(n, groups):
        if n == 0:
            for t in range(4):
                hand_out(t)
            cells_ref[HALF:, :] = cells_ref[HALF:, :] - product(below_ref[...], made[:HALF, :])
        elif n == 1:
            multiply(groups, 0, 2 * ORB)
        elif n == 2:
            hand_out(4)
            hand_out(5)
            multiply(groups, 2 * ORB, 3 * ORB)
        else:
            hand_out(6)
            multiply(groups, 3 * ORB, 4 * ORB)
            hand_out(7)

    @pl.when(jnp.logical_not(has_plane))
    def _():
        for i in range(2):
            bytes_of(z_in, 7, 2, i).wait_send()
            bytes_of(margin_ref, 12, 3, i).wait_send()

    @pl.when(has_plane)
    def _():
        bytes_of(margin_ref, 15, 3, 0).wait_recv()
        work[0] = block(0)
        first = jnp.concatenate(eliminate(groups_of(0), HALF), axis=0)
        first = jnp.where(row >= lane, first, 0.0)
        bytes_of(margin_ref, 15, 3, 1).wait_recv()
        below = product(block(1), first, ((1,), (1,)))
        below_ref[...] = below
        work[1] = block(2) - product(below, below, ((1,), (1,)))
        made[:HALF, :] = product(first, cells_ref[:HALF, :])
        eliminate(groups_of(1), HALF, after_block)
        for i in range(2):
            bytes_of(z_in, 7, 2, i).wait_send()
            bytes_of(margin_ref, 11, 3, i).wait_send()

    for p in range(PLANES):
        @pl.when(band != p)
        def _():
            from_plane(p).wait_recv()

    @pl.when(has_plane)
    def _():
        for t in range(8):
            @pl.when(band != t)
            def _():
                to_rows(t).wait_send()


def on_device(orbitals, potential):
    dma = pltpu.SemaphoreType.DMA
    piece = (24, 128)
    in_vmem = pl.BlockSpec(memory_space=pltpu.VMEM)
    planes = pl.pallas_call(
        whole_kernel,
        out_shape=pltpu.VMEM((PLANES, ORB, WIDTH), F32),
        in_specs=[pl.BlockSpec(memory_space=pltpu.HBM)] * 3,
        out_specs=in_vmem,
        scratch_shapes=[
            pltpu.VMEM((PLANES, WIDTH), F32),
            pltpu.VMEM((WIDTH, WIDTH), F32),
            pltpu.VMEM((BANDS, WIDTH), F32),
            pltpu.VMEM((16,) + piece, F32),
            pltpu.VMEM((BANDS, WIDTH), F32),
            pltpu.VMEM((2, HALF, HALF), F32),
            pltpu.VMEM((HALF, HALF), F32),
            pltpu.VMEM((4, 3 * PLANES, ORB, WIDTH), F32),
            pltpu.VMEM((CHUNKS, PLANES, CORB, WIDTH), F32),
            pltpu.VMEM((16,) + piece, F32),
            pltpu.VMEM((2 * PLANES,) + piece, F32),
            pltpu.VMEM((4,) + piece, F32),
            pltpu.VMEM((8,) + piece, F32),
            dma((3, CHUNKS, 2)),
            dma((3, CHUNKS, 2)),
            dma((2,)),
            dma((3,)),
            dma((4, 2, 2)),
            dma((2, 8)),
        ],
        compiler_params=pltpu.CompilerParams(
            collective_id=0, has_side_effects=True, vmem_limit_bytes=54 * 1024 * 1024
        ),
        name="filter_orthonormalize",
    )(jnp.transpose(orbitals, (1, 0, 2)), potential, jnp.asarray(plane_matrix()))
    return jnp.transpose(planes, (1, 0, 2))


def solution(mesh):
    placed = (P("band", "dom", None), P("dom", None))
    return jax.shard_map(
        on_device, mesh=mesh, in_specs=placed, out_specs=P("band", "dom", None), check_vma=False
    )
```

```python
import jax
import jax.numpy as jnp
import numpy as np
from jax import lax
from jax.experimental import pallas as pl
from jax.experimental.pallas import tpu as pltpu
from jax.sharding import PartitionSpec as P

NX = 16
ORB = 32
BANDS = 256
PLANES = 6
WIDTH = 256
CELLS = 98304
GROUPS = 8
CHUNKS = 4
CORB = ORB // CHUNKS
PIVOTS = 4
HALF = BANDS // 2

weights = (
    -5369.0 / 1800.0,
    12.0 / 7.0,
    -15.0 / 56.0,
    10.0 / 189.0,
    -1.0 / 112.0,
    2.0 / 1925.0,
    -1.0 / 16632.0,
)
centre = 6.0
half_width = 5.0
along_z = [-0.5 * w / half_width for w in weights]

FAR_BAND = (2, 6, 3, 5, 1, 7, 4)
FAR_HI = (2, 1, 3)
FAR_Z = (4, 3, 5, 2, 6, 1, 7)
MESH = pl.DeviceIdType.MESH
EXACT = lax.Precision.HIGHEST
F32 = jnp.float32


def plane_matrix():
    out = np.zeros((WIDTH, WIDTH))
    for cell in range(WIDTH):
        y, x = divmod(cell, NX)
        out[cell, cell] += 3.0 * weights[0]
        for step in range(1, 7):
            for sign in (-1, 1):
                out[(y + sign * step) % NX * NX + x, cell] += weights[step]
                out[y * NX + (x + sign * step) % NX, cell] += weights[step]
    return (-0.5 / half_width * out).astype(np.float32)


def product(a, b, dims=((1,), (0,))):
    return lax.dot_general(
        a, b, (dims, ((), ())), precision=EXACT, preferred_element_type=F32
    )


def greet(partners):
    barrier = pltpu.get_barrier_semaphore()
    for partner in partners:
        pl.semaphore_signal(barrier, inc=1, device_id=partner, device_id_type=MESH)
    pl.semaphore_wait(barrier, len(partners))


def send(src, dst, send_sem, recv_sem, device):
    copy = pltpu.make_async_remote_copy(
        src_ref=src,
        dst_ref=dst,
        send_sem=send_sem,
        recv_sem=recv_sem,
        device_id=device,
        device_id_type=MESH,
    )
    return copy


def eliminate(groups, size, after_rows=None):
    lane = lax.broadcasted_iota(jnp.int32, (8, size), 1)
    sublane = lax.broadcasted_iota(jnp.int32, (8, size), 0)
    groups = list(groups)
    span = range(PIVOTS)

    def spread_lane(tile, at):
        return jnp.broadcast_to(tile[:, at:at + 1], (8, size))

    def spread_row(tile, at):
        return jnp.broadcast_to(tile[at:at + 1, :], (8, size))

    entry = None
    for first in range(0, size, PIVOTS):
        home, off = divmod(first, 8)
        live = range(home, size // 8)
        columns = [{g: spread_lane(groups[g], first + q) for g in live} for q in span]
        if entry is None:
            entry = [[spread_row(columns[q][home], off + p) for q in range(p + 1)] for p in span]
        following = first + PIVOTS
        if following < size:
            near, near_off = divmod(following, 8)
            ahead = [spread_lane(groups[near], following + q) for q in span]
            ahead = [[spread_row(ahead[q], near_off + p) for q in range(p + 1)] for p in span]
            coupling = [[spread_row(columns[t][near], near_off + p) for t in span] for p in span]
        inside = (lane >= first) & (lane < following)
        scales = []
        low = [[None] * PIVOTS for _ in span]
        for q in span:
            value = entry[q][q]
            for t in range(q):
                value = value - low[q][t] * low[q][t]
            scales.append(lax.rsqrt(value))
            for p in range(q + 1, PIVOTS):
                value = entry[p][q]
                for t in range(q):
                    value = value - low[p][t] * low[q][t]
                low[p][q] = value * scales[q]
        if following < size:
            for t in span:
                for p in span:
                    value = coupling[p][t]
                    for u in range(t):
                        value = value - low[t][u] * coupling[p][u]
                    coupling[p][t] = value * scales[t]
            for p in span:
                for q in range(p + 1):
                    value = ahead[p][q]
                    for t in span:
                        value = value - coupling[p][t] * coupling[q][t]
                    ahead[p][q] = value
            entry = ahead
        scaled = []
        pivot_rows = []
        for q in span:
            column = dict(columns[q])
            row = spread_row(groups[home], off + q)
            row = jnp.where(inside, jnp.where(lane == first + q, 1.0, 0.0), row)
            for t in range(q):
                row = row - low[q][t] * pivot_rows[t]
                for g in live:
                    column[g] = column[g] - low[q][t] * scaled[t][g]
            pivot_rows.append(row * scales[q])
            scaled.append({g: column[g] * scales[q] for g in live})
        for g in live:
            if g == home and following % 8 == 0:
                new = groups[g]
            else:
                new = jnp.where(inside, 0.0, groups[g])
                for q in span:
                    new = new - scaled[q][g] * pivot_rows[q]
                if g == home:
                    new = jnp.where(sublane < off, groups[g], new)
            if g == home:
                for q in span:
                    new = jnp.where(sublane == off + q, pivot_rows[q], new)
            groups[g] = new
        if after_rows is not None:
            after_rows(following, groups)
    return groups


def rows_of(b):
    return pl.ds(pl.multiple_of(b * ORB, ORB), ORB)


def whole_kernel(x_ref, pot_hbm, mat_hbm, out_ref, pot_ref, mat_ref, cells_ref, margin_ref, made, work, below_ref,
                 field, local, part, band_in, hi_in, z_in,
                 halo_send, halo_recv, cell_sems, load_sems, sems, row_sems):
    band = lax.axis_index("band")
    dom = lax.axis_index("dom")
    count = lax.axis_size("dom")
    core = lax.rem(dom, 2)
    hi = lax.rem(lax.div(dom, 2), 4)
    z = lax.div(dom, 8)
    left = (band, lax.rem(dom + count - 1, count))
    right = (band, lax.rem(dom + 1, count))
    bands = [lax.rem(band + k, 8) for k in range(8)]
    senders = [lax.rem(band + 8 - k, 8) for k in range(8)]
    to_band = [(bands[k], dom) for k in range(8)]
    to_hi = [(band, z * 8 + lax.rem(hi + k, 4) * 2 + core) for k in range(4)]
    to_z = [(band, lax.rem(z + k, 8) * 8 + hi * 2 + core) for k in range(8)]
    has_plane = band < PLANES
    loads = [
        pltpu.make_async_copy(x_ref, field.at[0, pl.ds(PLANES, PLANES)], load_sems.at[0]),
        pltpu.make_async_copy(mat_hbm, mat_ref, load_sems.at[1]),
        pltpu.make_async_copy(pot_hbm, pot_ref, load_sems.at[2]),
    ]
    for load in loads:
        load.start()
    to_sixteen = [
        (k, flip, (bands[k], dom + flip * (1 - 2 * core)))
        for k in FAR_BAND + (0,) for flip in range(2) if k + flip > 0
    ]
    own = core * 8 + band
    greet([to_z[k] for k in FAR_Z] + [to_hi[k] for k in FAR_HI] + [left, right]
          + [where for _, _, where in to_sixteen])

    def chunk(c):
        return pl.ds(c * CORB, CORB)

    def halo(r, c):
        if r == 0:
            own = x_ref.at[:, chunk(c)]
        else:
            own = field.at[r, pl.ds(PLANES, PLANES), chunk(c)]
        return (
            send(own, field.at[r, pl.ds(2 * PLANES, PLANES), chunk(c)],
                 halo_send.at[r, c, 0], halo_recv.at[r, c, 0], left),
            send(own, field.at[r, pl.ds(0, PLANES), chunk(c)],
                 halo_send.at[r, c, 1], halo_recv.at[r, c, 1], right),
        )

    def in_plane(r, c):
        own = field[r, PLANES:2 * PLANES, c * CORB:(c + 1) * CORB, :]
        flat = own.reshape(PLANES * CORB, WIDTH)
        side = product(flat, mat_ref[...]).reshape(PLANES, CORB, WIDTH)
        for p in range(PLANES):
            diag = (pot_ref[p:p + 1, :] - centre) * (1.0 / half_width)
            local[c, p] = side[p] + diag * own[p]

    def rows_in(c):
        return pl.ds(pl.multiple_of(band * ORB, ORB) + c * CORB, CORB)

    def to_plane(k, c):
        return send(field.at[3, PLANES + bands[k], chunk(c)], cells_ref.at[rows_in(c)],
                    cell_sems.at[0], cell_sems.at[1], to_band[k])

    def all_planes():
        others = cells_ref.at[pl.ds(0, BANDS - ORB)]
        return send(others, others, cell_sems.at[0], cell_sems.at[1], to_band[1])

    for c in range(CHUNKS):
        for copy in halo(0, c):
            copy.start()
    for load in loads:
        load.wait()
    for c in range(CHUNKS):
        in_plane(0, c)
    for r in range(3):
        for c in range(CHUNKS):
            rows = slice(c * CORB, (c + 1) * CORB)
            for copy in halo(r, c):
                copy.wait_recv()
            for p in range(PLANES):
                total = local[c, p]
                for step in range(1, 7):
                    total = total + along_z[step] * (
                        field[r, PLANES + p - step, rows, :] + field[r, PLANES + p + step, rows, :]
                    )
                if r > 0:
                    total = 2.0 * total - field[r - 1, PLANES + p, rows, :]
                field[r + 1, PLANES + p, rows, :] = total
            if r < 2:
                for copy in halo(r + 1, c):
                    copy.start()
                in_plane(r + 1, c)
            else:
                for k in FAR_BAND:
                    @pl.when(bands[k] < PLANES)
                    def _():
                        to_plane(k, c).start()

                @pl.when(has_plane)
                def _():
                    cells_ref[rows_in(c), :] = field[3, PLANES + band, rows, :]

    def sixteenth(k, flip):
        return (core + flip * (1 - 2 * core)) * 8 + bands[k]

    parts = (pl.ds(0, 8), pl.ds(8, 16))

    def total_of(ref, count, i):
        total = ref[0, parts[i], :]
        for t in range(1, count):
            total = total + ref[t, parts[i], :]
        return total

    def bytes_of(ref, count, stage, i):
        some = ref.at[pl.ds(0, count), parts[i]]
        return send(some, some, sems.at[stage, 0, i], sems.at[stage, 1, i], left)

    def to_owner(k, flip, where, i):
        return send(part.at[sixteenth(k, flip), parts[i]], band_in.at[core * PLANES + band, parts[i]],
                    sems.at[0, 0, i], sems.at[0, 1, i], where)

    @pl.when(has_plane)
    def _():
        all_planes().wait_recv()
        for i in range(2):
            if i == 0:
                blocks = (product(cells_ref[:HALF, :], cells_ref[:HALF, :], ((1,), (1,))),)
            else:
                both = product(cells_ref[HALF:, :], cells_ref[...], ((1,), (1,)))
                blocks = (both[:, :HALF], both[:, HALF:])
            for q in range(16):
                for n, piece in enumerate(blocks):
                    part[q, 8 * (i + n):8 * (i + n) + 8, :] = piece[8 * q:8 * q + 8, :]
            for target in to_sixteen:
                to_owner(*target, i).start()
            band_in[core * PLANES + band, parts[i], :] = part[own, parts[i], :]

    def across_hi(k, i):
        mine = hi_in.at[hi, parts[i]]
        return send(mine, mine, sems.at[1, 0, i], sems.at[1, 1, i], to_hi[k])

    for i in range(2):
        @pl.when(has_plane)
        def _():
            bytes_of(band_in, 11, 0, i).wait_recv()

        @pl.when(jnp.logical_not(has_plane))
        def _():
            bytes_of(band_in, 12, 0, i).wait_recv()

        hi_in[hi, parts[i], :] = total_of(band_in, 12, i)
        for k in FAR_HI:
            across_hi(k, i).start()

    def across_z(k, i):
        mine = z_in.at[z, parts[i]]
        return send(mine, mine, sems.at[2, 0, i], sems.at[2, 1, i], to_z[k])

    def sent_planes(count):
        out = field.at[3, pl.ds(PLANES, count)]
        return send(out, out, cell_sems.at[0], cell_sems.at[1], left)

    def filter_sent():
        for c in range(CHUNKS):
            for r in range(3):
                for copy in halo(r, c):
                    copy.wait_send()

        @pl.when(jnp.logical_not(has_plane))
        def _():
            sent_planes(PLANES).wait_send()

        @pl.when(has_plane)
        def _():
            sent_planes(PLANES - 1).wait_send()
            for i in range(2):
                bytes_of(part, 15, 0, i).wait_send()

    for i in range(2):
        bytes_of(hi_in, 3, 1, i).wait_recv()
        z_in[z, parts[i], :] = total_of(hi_in, 4, i)
        for k in FAR_Z:
            across_z(k, i).start()
        if i == 0:
            filter_sent()

    def gather(where, i):
        mine = margin_ref.at[own, parts[i]]
        return send(mine, mine, sems.at[3, 0, i], sems.at[3, 1, i], where)

    for i in range(2):
        bytes_of(hi_in, 3, 1, i).wait_send()
        bytes_of(z_in, 7, 2, i).wait_recv()
        margin_ref[own, parts[i], :] = total_of(z_in, 8, i) * F32(1.0 / CELLS)
        for k, flip, where in to_sixteen:
            @pl.when(bands[k] < PLANES)
            def _():
                gather(where, i).start()

    def to_rows(t, begin=0, count=ORB):
        return send(made.at[pl.ds(t * ORB + begin, count)], out_ref.at[band, pl.ds(begin, count)],
                    row_sems.at[0, t], row_sems.at[1, band], (t, dom))

    def from_plane(p):
        return send(made.at[rows_of(0)], out_ref.at[p],
                    row_sems.at[0, 0], row_sems.at[1, p], (p, dom))

    lane = lax.broadcasted_iota(jnp.int32, (HALF, HALF), 1)
    row = lax.broadcasted_iota(jnp.int32, (HALF, HALF), 0)

    def block(i):
        return jnp.concatenate([margin_ref[q, 8 * i:8 * i + 8, :] for q in range(16)], axis=0)

    def groups_of(at):
        return [work[at, 8 * g:8 * g + 8, :] for g in range(HALF // 8)]

    def hand_out(t, begin=0, count=ORB):
        @pl.when(band != t)
        def _():
            to_rows(t, begin, count).start()

        @pl.when(band == t)
        def _():
            out_ref[t, begin:begin + count, :] = made[t * ORB + begin:t * ORB + begin + count, :]

    def multiply(groups, begin, end):
        rows = jnp.concatenate(groups[begin // 8:end // 8], axis=0)
        rows = jnp.where(row[begin:end] >= lane[begin:end], rows, 0.0)
        made[HALF + begin:HALF + end, :] = product(rows, cells_ref[HALF:, :])

    def after_rows(n, groups):
        if n == 32:
            for t in range(4):
                hand_out(t)
            cells_ref[HALF:, :] = cells_ref[HALF:, :] - product(below_ref[...], made[:HALF, :])
        elif n == 64:
            multiply(groups, 0, 64)
        elif n == 96:
            hand_out(4)
            hand_out(5)
            multiply(groups, 64, 96)
        elif n == 112:
            hand_out(6)
            multiply(groups, 96, 112)
        elif n == 128:
            hand_out(7, 0, 16)
            multiply(groups, 112, 128)
            hand_out(7, 16, 16)

    @pl.when(jnp.logical_not(has_plane))
    def _():
        for i in range(2):
            bytes_of(z_in, 7, 2, i).wait_send()
            bytes_of(margin_ref, 12, 3, i).wait_send()

    @pl.when(has_plane)
    def _():
        bytes_of(margin_ref, 15, 3, 0).wait_recv()
        work[0] = block(0)
        first = jnp.concatenate(eliminate(groups_of(0), HALF), axis=0)
        first = jnp.where(row >= lane, first, 0.0)
        bytes_of(margin_ref, 15, 3, 1).wait_recv()
        below = product(block(1), first, ((1,), (1,)))
        below_ref[...] = below
        work[1] = block(2) - product(below, below, ((1,), (1,)))
        made[:HALF, :] = product(first, cells_ref[:HALF, :])
        eliminate(groups_of(1), HALF, after_rows)
        for i in range(2):
            bytes_of(z_in, 7, 2, i).wait_send()
            bytes_of(margin_ref, 11, 3, i).wait_send()

    for p in range(PLANES):
        @pl.when(band != p)
        def _():
            from_plane(p).wait_recv()

    @pl.when(has_plane)
    def _():
        for t in range(8):
            @pl.when(band != t)
            def _():
                to_rows(t).wait_send()


def on_device(orbitals, potential):
    dma = pltpu.SemaphoreType.DMA
    piece = (24, 128)
    in_vmem = pl.BlockSpec(memory_space=pltpu.VMEM)
    planes = pl.pallas_call(
        whole_kernel,
        out_shape=pltpu.VMEM((PLANES, ORB, WIDTH), F32),
        in_specs=[pl.BlockSpec(memory_space=pltpu.HBM)] * 3,
        out_specs=in_vmem,
        scratch_shapes=[
            pltpu.VMEM((PLANES, WIDTH), F32),
            pltpu.VMEM((WIDTH, WIDTH), F32),
            pltpu.VMEM((BANDS, WIDTH), F32),
            pltpu.VMEM((16,) + piece, F32),
            pltpu.VMEM((BANDS, WIDTH), F32),
            pltpu.VMEM((2, HALF, HALF), F32),
            pltpu.VMEM((HALF, HALF), F32),
            pltpu.VMEM((4, 3 * PLANES, ORB, WIDTH), F32),
            pltpu.VMEM((CHUNKS, PLANES, CORB, WIDTH), F32),
            pltpu.VMEM((16,) + piece, F32),
            pltpu.VMEM((2 * PLANES,) + piece, F32),
            pltpu.VMEM((4,) + piece, F32),
            pltpu.VMEM((8,) + piece, F32),
            dma((3, CHUNKS, 2)),
            dma((3, CHUNKS, 2)),
            dma((2,)),
            dma((3,)),
            dma((4, 2, 2)),
            dma((2, 8)),
        ],
        compiler_params=pltpu.CompilerParams(
            collective_id=0, has_side_effects=True, vmem_limit_bytes=54 * 1024 * 1024
        ),
        name="filter_orthonormalize",
    )(jnp.transpose(orbitals, (1, 0, 2)), potential, jnp.asarray(plane_matrix()))
    return jnp.transpose(planes, (1, 0, 2))


def solution(mesh):
    placed = (P("band", "dom", None), P("dom", None))
    return jax.shard_map(
        on_device, mesh=mesh, in_specs=placed, out_specs=P("band", "dom", None), check_vma=False
    )
```

```python
import jax
import jax.numpy as jnp
import numpy as np
from jax import lax
from jax.experimental import pallas as pl
from jax.experimental.pallas import tpu as pltpu
from jax.sharding import PartitionSpec as P

NX = 16
ORB = 32
BANDS = 256
PLANES = 6
WIDTH = 256
CELLS = 98304
GROUPS = 8
CHUNKS = 4
CORB = ORB // CHUNKS
PIVOTS = 4
HALF = BANDS // 2

weights = (
    -5369.0 / 1800.0,
    12.0 / 7.0,
    -15.0 / 56.0,
    10.0 / 189.0,
    -1.0 / 112.0,
    2.0 / 1925.0,
    -1.0 / 16632.0,
)
centre = 6.0
half_width = 5.0
along_z = [-0.5 * w / half_width for w in weights]

FAR_BAND = (2, 6, 3, 5, 1, 7, 4)
FAR_HI = (2, 1, 3)
FAR_Z = (4, 3, 5, 2, 6, 1, 7)
MESH = pl.DeviceIdType.MESH
EXACT = lax.Precision.HIGHEST
F32 = jnp.float32


def plane_matrix():
    out = np.zeros((WIDTH, WIDTH))
    for cell in range(WIDTH):
        y, x = divmod(cell, NX)
        out[cell, cell] += 3.0 * weights[0]
        for step in range(1, 7):
            for sign in (-1, 1):
                out[(y + sign * step) % NX * NX + x, cell] += weights[step]
                out[y * NX + (x + sign * step) % NX, cell] += weights[step]
    return (-0.5 / half_width * out).astype(np.float32)


def product(a, b, dims=((1,), (0,))):
    return lax.dot_general(
        a, b, (dims, ((), ())), precision=EXACT, preferred_element_type=F32
    )


def greet(partners):
    barrier = pltpu.get_barrier_semaphore()
    for partner in partners:
        pl.semaphore_signal(barrier, inc=1, device_id=partner, device_id_type=MESH)
    pl.semaphore_wait(barrier, len(partners))


def send(src, dst, send_sem, recv_sem, device):
    copy = pltpu.make_async_remote_copy(
        src_ref=src,
        dst_ref=dst,
        send_sem=send_sem,
        recv_sem=recv_sem,
        device_id=device,
        device_id_type=MESH,
    )
    return copy


def eliminate(groups, size, after_rows=None):
    lane = lax.broadcasted_iota(jnp.int32, (8, size), 1)
    sublane = lax.broadcasted_iota(jnp.int32, (8, size), 0)
    groups = list(groups)
    span = range(PIVOTS)

    def spread_lane(tile, at):
        return jnp.broadcast_to(tile[:, at:at + 1], (8, size))

    def spread_row(tile, at):
        return jnp.broadcast_to(tile[at:at + 1, :], (8, size))

    entry = None
    for first in range(0, size, PIVOTS):
        home, off = divmod(first, 8)
        live = range(home, size // 8)
        columns = [{g: spread_lane(groups[g], first + q) for g in live} for q in span]
        if entry is None:
            entry = [[spread_row(columns[q][home], off + p) for q in range(p + 1)] for p in span]
        following = first + PIVOTS
        if following < size:
            near, near_off = divmod(following, 8)
            ahead = [spread_lane(groups[near], following + q) for q in span]
            ahead = [[spread_row(ahead[q], near_off + p) for q in range(p + 1)] for p in span]
            coupling = [[spread_row(columns[t][near], near_off + p) for t in span] for p in span]
        inside = (lane >= first) & (lane < following)
        scales = []
        low = [[None] * PIVOTS for _ in span]
        for q in span:
            value = entry[q][q]
            for t in range(q):
                value = value - low[q][t] * low[q][t]
            scales.append(lax.rsqrt(value))
            for p in range(q + 1, PIVOTS):
                value = entry[p][q]
                for t in range(q):
                    value = value - low[p][t] * low[q][t]
                low[p][q] = value * scales[q]
        if following < size:
            for t in span:
                for p in span:
                    value = coupling[p][t]
                    for u in range(t):
                        value = value - low[t][u] * coupling[p][u]
                    coupling[p][t] = value * scales[t]
            for p in span:
                for q in range(p + 1):
                    value = ahead[p][q]
                    for t in span:
                        value = value - coupling[p][t] * coupling[q][t]
                    ahead[p][q] = value
            entry = ahead
        scaled = []
        pivot_rows = []
        for q in span:
            column = dict(columns[q])
            row = spread_row(groups[home], off + q)
            row = jnp.where(inside, jnp.where(lane == first + q, 1.0, 0.0), row)
            for t in range(q):
                row = row - low[q][t] * pivot_rows[t]
                for g in live:
                    column[g] = column[g] - low[q][t] * scaled[t][g]
            pivot_rows.append(row * scales[q])
            scaled.append({g: column[g] * scales[q] for g in live})
        for g in live:
            if g == home and following % 8 == 0:
                new = groups[g]
            else:
                new = jnp.where(inside, 0.0, groups[g])
                for q in span:
                    new = new - scaled[q][g] * pivot_rows[q]
                if g == home:
                    new = jnp.where(sublane < off, groups[g], new)
            if g == home:
                for q in span:
                    new = jnp.where(sublane == off + q, pivot_rows[q], new)
            groups[g] = new
        if after_rows is not None:
            after_rows(following, groups)
    return groups


def rows_of(b):
    return pl.ds(pl.multiple_of(b * ORB, ORB), ORB)


def whole_kernel(x_ref, pot_hbm, mat_hbm, out_ref, pot_ref, mat_ref, cells_ref, margin_ref, made, work, below_ref,
                 field, local, part, band_in, hi_in, z_in,
                 halo_send, halo_recv, cell_sems, load_sems, sems, row_sems):
    band = lax.axis_index("band")
    dom = lax.axis_index("dom")
    count = lax.axis_size("dom")
    core = lax.rem(dom, 2)
    hi = lax.rem(lax.div(dom, 2), 4)
    z = lax.div(dom, 8)
    left = (band, lax.rem(dom + count - 1, count))
    right = (band, lax.rem(dom + 1, count))
    bands = [lax.rem(band + k, 8) for k in range(8)]
    senders = [lax.rem(band + 8 - k, 8) for k in range(8)]
    to_band = [(bands[k], dom) for k in range(8)]
    to_hi = [(band, z * 8 + lax.rem(hi + k, 4) * 2 + core) for k in range(4)]
    to_z = [(band, lax.rem(z + k, 8) * 8 + hi * 2 + core) for k in range(8)]
    has_plane = band < PLANES
    loads = [
        pltpu.make_async_copy(x_ref, field.at[0, pl.ds(PLANES, PLANES)], load_sems.at[0]),
        pltpu.make_async_copy(mat_hbm, mat_ref, load_sems.at[1]),
        pltpu.make_async_copy(pot_hbm, pot_ref, load_sems.at[2]),
    ]
    for load in loads:
        load.start()
    to_sixteen = [
        (k, flip, (bands[k], dom + flip * (1 - 2 * core)))
        for k in FAR_BAND + (0,) for flip in range(2) if k + flip > 0
    ]
    own = core * 8 + band
    greet([to_z[k] for k in FAR_Z] + [to_hi[k] for k in FAR_HI] + [left, right]
          + [where for _, _, where in to_sixteen])

    def chunk(c):
        return pl.ds(c * CORB, CORB)

    def halo(r, c, h):
        side = pl.ds(h * 128, 128)
        own = field.at[r, pl.ds(PLANES, PLANES), chunk(c), side]
        return (
            send(own, field.at[r, pl.ds(2 * PLANES, PLANES), chunk(c), side],
                 halo_send.at[r, c, h, 0], halo_recv.at[r, c, h, 0], left),
            send(own, field.at[r, pl.ds(0, PLANES), chunk(c), side],
                 halo_send.at[r, c, h, 1], halo_recv.at[r, c, h, 1], right),
        )

    def in_plane(r, c):
        own = field[r, PLANES:2 * PLANES, c * CORB:(c + 1) * CORB, :]
        flat = own.reshape(PLANES * CORB, WIDTH)
        side = product(flat, mat_ref[...]).reshape(PLANES, CORB, WIDTH)
        for p in range(PLANES):
            diag = (pot_ref[p:p + 1, :] - centre) * (1.0 / half_width)
            local[c, p] = side[p] + diag * own[p]

    def rows_in(c):
        return pl.ds(pl.multiple_of(band * ORB, ORB) + c * CORB, CORB)

    def to_plane(k, c):
        return send(field.at[3, PLANES + bands[k], chunk(c)], cells_ref.at[rows_in(c)],
                    cell_sems.at[0], cell_sems.at[1], to_band[k])

    def all_planes():
        others = cells_ref.at[pl.ds(0, BANDS - ORB)]
        return send(others, others, cell_sems.at[0], cell_sems.at[1], to_band[1])

    for load in loads:
        load.wait()
    for c in range(CHUNKS):
        for h in range(2):
            for copy in halo(0, c, h):
                copy.start()
    for c in range(CHUNKS):
        in_plane(0, c)
    for r in range(3):
        for c in range(CHUNKS):
            rows = slice(c * CORB, (c + 1) * CORB)
            for h in range(2):
                side = slice(h * 128, (h + 1) * 128)
                for copy in halo(r, c, h):
                    copy.wait_recv()
                for p in range(PLANES):
                    total = local[c, p, :, side]
                    for step in range(1, 7):
                        total = total + along_z[step] * (
                            field[r, PLANES + p - step, rows, side] + field[r, PLANES + p + step, rows, side]
                        )
                    if r > 0:
                        total = 2.0 * total - field[r - 1, PLANES + p, rows, side]
                    field[r + 1, PLANES + p, rows, side] = total
                if r < 2:
                    for copy in halo(r + 1, c, h):
                        copy.start()
            if r < 2:
                in_plane(r + 1, c)
            else:
                for k in FAR_BAND:
                    @pl.when(bands[k] < PLANES)
                    def _():
                        to_plane(k, c).start()

                @pl.when(has_plane)
                def _():
                    cells_ref[rows_in(c), :] = field[3, PLANES + band, rows, :]

    def sixteenth(k, flip):
        return (core + flip * (1 - 2 * core)) * 8 + bands[k]

    parts = (pl.ds(0, 8), pl.ds(8, 16))

    def total_of(ref, count, i):
        total = ref[0, parts[i], :]
        for t in range(1, count):
            total = total + ref[t, parts[i], :]
        return total

    def bytes_of(ref, count, stage, i):
        some = ref.at[pl.ds(0, count), parts[i]]
        return send(some, some, sems.at[stage, 0, i], sems.at[stage, 1, i], left)

    def to_owner(k, flip, where, i):
        return send(part.at[sixteenth(k, flip), parts[i]], band_in.at[core * PLANES + band, parts[i]],
                    sems.at[0, 0, i], sems.at[0, 1, i], where)

    @pl.when(has_plane)
    def _():
        all_planes().wait_recv()
        for i in range(2):
            if i == 0:
                blocks = (product(cells_ref[:HALF, :], cells_ref[:HALF, :], ((1,), (1,))),)
            else:
                both = product(cells_ref[HALF:, :], cells_ref[...], ((1,), (1,)))
                blocks = (both[:, :HALF], both[:, HALF:])
            for q in range(16):
                for n, piece in enumerate(blocks):
                    part[q, 8 * (i + n):8 * (i + n) + 8, :] = piece[8 * q:8 * q + 8, :]
            for target in to_sixteen:
                to_owner(*target, i).start()
            band_in[core * PLANES + band, parts[i], :] = part[own, parts[i], :]

    def across_hi(k, i):
        mine = hi_in.at[hi, parts[i]]
        return send(mine, mine, sems.at[1, 0, i], sems.at[1, 1, i], to_hi[k])

    for i in range(2):
        @pl.when(has_plane)
        def _():
            bytes_of(band_in, 11, 0, i).wait_recv()

        @pl.when(jnp.logical_not(has_plane))
        def _():
            bytes_of(band_in, 12, 0, i).wait_recv()

        hi_in[hi, parts[i], :] = total_of(band_in, 12, i)
        for k in FAR_HI:
            across_hi(k, i).start()

    def across_z(k, i):
        mine = z_in.at[z, parts[i]]
        return send(mine, mine, sems.at[2, 0, i], sems.at[2, 1, i], to_z[k])

    def sent_planes(count):
        out = field.at[3, pl.ds(PLANES, count)]
        return send(out, out, cell_sems.at[0], cell_sems.at[1], left)

    def filter_sent():
        for c in range(CHUNKS):
            for r in range(3):
                for h in range(2):
                    for copy in halo(r, c, h):
                        copy.wait_send()

        @pl.when(jnp.logical_not(has_plane))
        def _():
            sent_planes(PLANES).wait_send()

        @pl.when(has_plane)
        def _():
            sent_planes(PLANES - 1).wait_send()
            for i in range(2):
                bytes_of(part, 15, 0, i).wait_send()

    for i in range(2):
        bytes_of(hi_in, 3, 1, i).wait_recv()
        z_in[z, parts[i], :] = total_of(hi_in, 4, i)
        for k in FAR_Z:
            across_z(k, i).start()
        if i == 0:
            filter_sent()

    def gather(where, i):
        mine = margin_ref.at[own, parts[i]]
        return send(mine, mine, sems.at[3, 0, i], sems.at[3, 1, i], where)

    for i in range(2):
        bytes_of(hi_in, 3, 1, i).wait_send()
        bytes_of(z_in, 7, 2, i).wait_recv()
        margin_ref[own, parts[i], :] = total_of(z_in, 8, i) * F32(1.0 / CELLS)
        for k, flip, where in to_sixteen:
            @pl.when(bands[k] < PLANES)
            def _():
                gather(where, i).start()

    def to_rows(t, begin=0, count=ORB):
        return send(made.at[pl.ds(t * ORB + begin, count)], out_ref.at[band, pl.ds(begin, count)],
                    row_sems.at[0, t], row_sems.at[1, band], (t, dom))

    def from_plane(p):
        return send(made.at[rows_of(0)], out_ref.at[p],
                    row_sems.at[0, 0], row_sems.at[1, p], (p, dom))

    lane = lax.broadcasted_iota(jnp.int32, (HALF, HALF), 1)
    row = lax.broadcasted_iota(jnp.int32, (HALF, HALF), 0)

    def block(i):
        return jnp.concatenate([margin_ref[q, 8 * i:8 * i + 8, :] for q in range(16)], axis=0)

    def groups_of(at):
        return [work[at, 8 * g:8 * g + 8, :] for g in range(HALF // 8)]

    def hand_out(t, begin=0, count=ORB):
        @pl.when(band != t)
        def _():
            to_rows(t, begin, count).start()

        @pl.when(band == t)
        def _():
            out_ref[t, begin:begin + count, :] = made[t * ORB + begin:t * ORB + begin + count, :]

    def multiply(groups, begin, end):
        rows = jnp.concatenate(groups[begin // 8:end // 8], axis=0)
        rows = jnp.where(row[begin:end] >= lane[begin:end], rows, 0.0)
        made[HALF + begin:HALF + end, :] = product(rows, cells_ref[HALF:, :])

    def after_rows(n, groups):
        if n == 32:
            for t in range(4):
                hand_out(t)
            cells_ref[HALF:, :] = cells_ref[HALF:, :] - product(below_ref[...], made[:HALF, :])
        elif n == 64:
            multiply(groups, 0, 64)
        elif n == 96:
            hand_out(4)
            hand_out(5)
            multiply(groups, 64, 96)
        elif n == 112:
            hand_out(6)
            multiply(groups, 96, 112)
        elif n == 128:
            hand_out(7, 0, 16)
            multiply(groups, 112, 128)
            hand_out(7, 16, 16)

    @pl.when(jnp.logical_not(has_plane))
    def _():
        for i in range(2):
            bytes_of(z_in, 7, 2, i).wait_send()
            bytes_of(margin_ref, 12, 3, i).wait_send()

    @pl.when(has_plane)
    def _():
        bytes_of(margin_ref, 15, 3, 0).wait_recv()
        work[0] = block(0)
        first = jnp.concatenate(eliminate(groups_of(0), HALF), axis=0)
        first = jnp.where(row >= lane, first, 0.0)
        bytes_of(margin_ref, 15, 3, 1).wait_recv()
        below = product(block(1), first, ((1,), (1,)))
        below_ref[...] = below
        work[1] = block(2) - product(below, below, ((1,), (1,)))
        made[:HALF, :] = product(first, cells_ref[:HALF, :])
        eliminate(groups_of(1), HALF, after_rows)
        for i in range(2):
            bytes_of(z_in, 7, 2, i).wait_send()
            bytes_of(margin_ref, 11, 3, i).wait_send()

    for p in range(PLANES):
        @pl.when(band != p)
        def _():
            from_plane(p).wait_recv()

    @pl.when(has_plane)
    def _():
        for t in range(8):
            @pl.when(band != t)
            def _():
                to_rows(t).wait_send()


def on_device(orbitals, potential):
    dma = pltpu.SemaphoreType.DMA
    piece = (24, 128)
    in_vmem = pl.BlockSpec(memory_space=pltpu.VMEM)
    planes = pl.pallas_call(
        whole_kernel,
        out_shape=pltpu.VMEM((PLANES, ORB, WIDTH), F32),
        in_specs=[pl.BlockSpec(memory_space=pltpu.HBM)] * 3,
        out_specs=in_vmem,
        scratch_shapes=[
            pltpu.VMEM((PLANES, WIDTH), F32),
            pltpu.VMEM((WIDTH, WIDTH), F32),
            pltpu.VMEM((BANDS, WIDTH), F32),
            pltpu.VMEM((16,) + piece, F32),
            pltpu.VMEM((BANDS, WIDTH), F32),
            pltpu.VMEM((2, HALF, HALF), F32),
            pltpu.VMEM((HALF, HALF), F32),
            pltpu.VMEM((4, 3 * PLANES, ORB, WIDTH), F32),
            pltpu.VMEM((CHUNKS, PLANES, CORB, WIDTH), F32),
            pltpu.VMEM((16,) + piece, F32),
            pltpu.VMEM((2 * PLANES,) + piece, F32),
            pltpu.VMEM((4,) + piece, F32),
            pltpu.VMEM((8,) + piece, F32),
            dma((3, CHUNKS, 2, 2)),
            dma((3, CHUNKS, 2, 2)),
            dma((2,)),
            dma((3,)),
            dma((4, 2, 2)),
            dma((2, 8)),
        ],
        compiler_params=pltpu.CompilerParams(
            collective_id=0, has_side_effects=True, vmem_limit_bytes=54 * 1024 * 1024
        ),
        name="filter_orthonormalize",
    )(jnp.transpose(orbitals, (1, 0, 2)), potential, jnp.asarray(plane_matrix()))
    return jnp.transpose(planes, (1, 0, 2))


def solution(mesh):
    placed = (P("band", "dom", None), P("dom", None))
    return jax.shard_map(
        on_device, mesh=mesh, in_specs=placed, out_specs=P("band", "dom", None), check_vma=False
    )
```

```python
import jax
import jax.numpy as jnp
import numpy as np
from jax import lax
from jax.experimental import pallas as pl
from jax.experimental.pallas import tpu as pltpu
from jax.sharding import PartitionSpec as P

NX = 16
ORB = 32
BANDS = 256
PLANES = 6
WIDTH = 256
CELLS = 98304
GROUPS = 8
CHUNKS = 4
CORB = ORB // CHUNKS
PIVOTS = 4
HALF = BANDS // 2

weights = (
    -5369.0 / 1800.0,
    12.0 / 7.0,
    -15.0 / 56.0,
    10.0 / 189.0,
    -1.0 / 112.0,
    2.0 / 1925.0,
    -1.0 / 16632.0,
)
centre = 6.0
half_width = 5.0
along_z = [-0.5 * w / half_width for w in weights]

FAR_BAND = (2, 6, 3, 5, 1, 7, 4)
FAR_HI = (2, 1, 3)
FAR_Z = (4, 3, 5, 2, 6, 1, 7)
MESH = pl.DeviceIdType.MESH
EXACT = lax.Precision.HIGHEST
F32 = jnp.float32


def plane_matrix():
    out = np.zeros((WIDTH, WIDTH))
    for cell in range(WIDTH):
        y, x = divmod(cell, NX)
        out[cell, cell] += 3.0 * weights[0]
        for step in range(1, 7):
            for sign in (-1, 1):
                out[(y + sign * step) % NX * NX + x, cell] += weights[step]
                out[y * NX + (x + sign * step) % NX, cell] += weights[step]
    return (-0.5 / half_width * out).astype(np.float32)


def product(a, b, dims=((1,), (0,))):
    return lax.dot_general(
        a, b, (dims, ((), ())), precision=EXACT, preferred_element_type=F32
    )


def greet(partners):
    barrier = pltpu.get_barrier_semaphore()
    for partner in partners:
        pl.semaphore_signal(barrier, inc=1, device_id=partner, device_id_type=MESH)
    pl.semaphore_wait(barrier, len(partners))


def send(src, dst, send_sem, recv_sem, device):
    copy = pltpu.make_async_remote_copy(
        src_ref=src,
        dst_ref=dst,
        send_sem=send_sem,
        recv_sem=recv_sem,
        device_id=device,
        device_id_type=MESH,
    )
    return copy


def eliminate(groups, size, after_rows=None):
    lane = lax.broadcasted_iota(jnp.int32, (8, size), 1)
    sublane = lax.broadcasted_iota(jnp.int32, (8, size), 0)
    groups = list(groups)
    span = range(PIVOTS)

    def spread_lane(tile, at):
        return jnp.broadcast_to(tile[:, at:at + 1], (8, size))

    def spread_row(tile, at):
        return jnp.broadcast_to(tile[at:at + 1, :], (8, size))

    entry = None
    for first in range(0, size, PIVOTS):
        home, off = divmod(first, 8)
        live = range(home, size // 8)
        columns = [{g: spread_lane(groups[g], first + q) for g in live} for q in span]
        if entry is None:
            entry = [[spread_row(columns[q][home], off + p) for q in range(p + 1)] for p in span]
        following = first + PIVOTS
        if following < size:
            near, near_off = divmod(following, 8)
            ahead = [spread_lane(groups[near], following + q) for q in span]
            ahead = [[spread_row(ahead[q], near_off + p) for q in range(p + 1)] for p in span]
            coupling = [[spread_row(columns[t][near], near_off + p) for t in span] for p in span]
        inside = (lane >= first) & (lane < following)
        scales = []
        low = [[None] * PIVOTS for _ in span]
        for q in span:
            value = entry[q][q]
            for t in range(q):
                value = value - low[q][t] * low[q][t]
            scales.append(lax.rsqrt(value))
            for p in range(q + 1, PIVOTS):
                value = entry[p][q]
                for t in range(q):
                    value = value - low[p][t] * low[q][t]
                low[p][q] = value * scales[q]
        if following < size:
            for t in span:
                for p in span:
                    value = coupling[p][t]
                    for u in range(t):
                        value = value - low[t][u] * coupling[p][u]
                    coupling[p][t] = value * scales[t]
            for p in span:
                for q in range(p + 1):
                    value = ahead[p][q]
                    for t in span:
                        value = value - coupling[p][t] * coupling[q][t]
                    ahead[p][q] = value
            entry = ahead
        scaled = []
        pivot_rows = []
        for q in span:
            column = dict(columns[q])
            row = spread_row(groups[home], off + q)
            row = jnp.where(inside, jnp.where(lane == first + q, 1.0, 0.0), row)
            for t in range(q):
                row = row - low[q][t] * pivot_rows[t]
                for g in live:
                    column[g] = column[g] - low[q][t] * scaled[t][g]
            pivot_rows.append(row * scales[q])
            scaled.append({g: column[g] * scales[q] for g in live})
        for g in live:
            if g == home and following % 8 == 0:
                new = groups[g]
            else:
                new = jnp.where(inside, 0.0, groups[g])
                for q in span:
                    new = new - scaled[q][g] * pivot_rows[q]
                if g == home:
                    new = jnp.where(sublane < off, groups[g], new)
            if g == home:
                for q in span:
                    new = jnp.where(sublane == off + q, pivot_rows[q], new)
            groups[g] = new
        if after_rows is not None:
            after_rows(following, groups)
    return groups


def rows_of(b):
    return pl.ds(pl.multiple_of(b * ORB, ORB), ORB)


def whole_kernel(x_ref, pot_hbm, mat_hbm, out_ref, pot_ref, mat_ref, cells_ref, margin_ref, made, work, below_ref,
                 field, local, part, band_in, hi_in, z_in,
                 halo_send, halo_recv, cell_sems, load_sems, sems, row_sems):
    band = lax.axis_index("band")
    dom = lax.axis_index("dom")
    count = lax.axis_size("dom")
    core = lax.rem(dom, 2)
    hi = lax.rem(lax.div(dom, 2), 4)
    z = lax.div(dom, 8)
    left = (band, lax.rem(dom + count - 1, count))
    right = (band, lax.rem(dom + 1, count))
    bands = [lax.rem(band + k, 8) for k in range(8)]
    to_band = [(bands[k], dom) for k in range(8)]
    to_hi = [(band, z * 8 + lax.rem(hi + k, 4) * 2 + core) for k in range(4)]
    to_z = [(band, lax.rem(z + k, 8) * 8 + hi * 2 + core) for k in range(8)]
    has_plane = band < PLANES
    loads = [
        pltpu.make_async_copy(x_ref, field.at[0, pl.ds(PLANES, PLANES)], load_sems.at[0]),
        pltpu.make_async_copy(mat_hbm, mat_ref, load_sems.at[1]),
        pltpu.make_async_copy(pot_hbm, pot_ref, load_sems.at[2]),
    ]
    for load in loads:
        load.start()
    to_sixteen = [
        (k, flip, (bands[k], dom + flip * (1 - 2 * core)))
        for k in FAR_BAND + (0,) for flip in range(2) if k + flip > 0
    ]
    greet([to_z[k] for k in FAR_Z] + [to_hi[k] for k in FAR_HI] + [left, right]
          + [where for _, _, where in to_sixteen])

    def chunk(c):
        return pl.ds(c * CORB, CORB)

    def halo(r, c):
        if r == 0:
            own = x_ref.at[:, chunk(c)]
        else:
            own = field.at[r, pl.ds(PLANES, PLANES), chunk(c)]
        return (
            send(own, field.at[r, pl.ds(2 * PLANES, PLANES), chunk(c)],
                 halo_send.at[r, c, 0], halo_recv.at[r, c, 0], left),
            send(own, field.at[r, pl.ds(0, PLANES), chunk(c)],
                 halo_send.at[r, c, 1], halo_recv.at[r, c, 1], right),
        )

    def in_plane(r, c):
        own = field[r, PLANES:2 * PLANES, c * CORB:(c + 1) * CORB, :]
        flat = own.reshape(PLANES * CORB, WIDTH)
        side = product(flat, mat_ref[...]).reshape(PLANES, CORB, WIDTH)
        for p in range(PLANES):
            diag = (pot_ref[p:p + 1, :] - centre) * (1.0 / half_width)
            local[c, p] = side[p] + diag * own[p]

    def rows_in(c):
        return pl.ds(pl.multiple_of(band * ORB, ORB) + c * CORB, CORB)

    def to_plane(k, c):
        return send(field.at[3, PLANES + bands[k], chunk(c)], cells_ref.at[rows_in(c)],
                    cell_sems.at[0], cell_sems.at[1], to_band[k])

    def all_planes():
        others = cells_ref.at[pl.ds(0, BANDS - ORB)]
        return send(others, others, cell_sems.at[0], cell_sems.at[1], to_band[1])

    for c in range(CHUNKS):
        for copy in halo(0, c):
            copy.start()
    for load in loads:
        load.wait()
    for c in range(CHUNKS):
        in_plane(0, c)
    for r in range(3):
        for c in range(CHUNKS):
            rows = slice(c * CORB, (c + 1) * CORB)
            for copy in halo(r, c):
                copy.wait_recv()
            for p in range(PLANES):
                total = local[c, p]
                for step in range(1, 7):
                    total = total + along_z[step] * (
                        field[r, PLANES + p - step, rows, :] + field[r, PLANES + p + step, rows, :]
                    )
                if r > 0:
                    total = 2.0 * total - field[r - 1, PLANES + p, rows, :]
                field[r + 1, PLANES + p, rows, :] = total
            if r < 2:
                for copy in halo(r + 1, c):
                    copy.start()
                in_plane(r + 1, c)
            else:
                for k in FAR_BAND:
                    @pl.when(bands[k] < PLANES)
                    def _():
                        to_plane(k, c).start()

                @pl.when(has_plane)
                def _():
                    cells_ref[rows_in(c), :] = field[3, PLANES + band, rows, :]

    parts = (pl.ds(0, 16), pl.ds(16, 32))

    def total_of(ref, count, i):
        total = ref[0, parts[i], :]
        for t in range(1, count):
            total = total + ref[t, parts[i], :]
        return total

    def bytes_of(ref, count, stage, i):
        some = ref.at[pl.ds(0, count), parts[i]]
        return send(some, some, sems.at[stage, 0, i], sems.at[stage, 1, i], left)

    def to_owner(k, i):
        return send(part.at[bands[k], parts[i]], band_in.at[core * PLANES + band, parts[i]],
                    sems.at[0, 0, i], sems.at[0, 1, i], (bands[k], dom - core + i))

    @pl.when(has_plane)
    def _():
        all_planes().wait_recv()
        for i in range(2):
            if i == 0:
                blocks = (product(cells_ref[:HALF, :], cells_ref[:HALF, :], ((1,), (1,))),)
            else:
                both = product(cells_ref[HALF:, :], cells_ref[...], ((1,), (1,)))
                blocks = (both[:, :HALF], both[:, HALF:])
            for q in range(8):
                for n, piece in enumerate(blocks):
                    part[q, 16 * (i + n):16 * (i + n) + 16, :] = piece[16 * q:16 * q + 16, :]
            for k in FAR_BAND:
                to_owner(k, i).start()

            @pl.when(core != i)
            def _():
                to_owner(0, i).start()

            @pl.when(core == i)
            def _():
                band_in[core * PLANES + band, parts[i], :] = part[band, parts[i], :]

    def across_hi(k, i):
        mine = hi_in.at[hi, parts[i]]
        return send(mine, mine, sems.at[1, 0, i], sems.at[1, 1, i], to_hi[k])

    def across_z(k, i):
        mine = z_in.at[z, parts[i]]
        return send(mine, mine, sems.at[2, 0, i], sems.at[2, 1, i], to_z[k])

    def sent_planes(count):
        out = field.at[3, pl.ds(PLANES, count)]
        return send(out, out, cell_sems.at[0], cell_sems.at[1], left)

    def filter_sent():
        for c in range(CHUNKS):
            for r in range(3):
                for copy in halo(r, c):
                    copy.wait_send()

        @pl.when(jnp.logical_not(has_plane))
        def _():
            sent_planes(PLANES).wait_send()

        @pl.when(has_plane)
        def _():
            sent_planes(PLANES - 1).wait_send()
            for i in range(2):
                @pl.when(core == i)
                def _():
                    bytes_of(part, 7, 0, i).wait_send()

                @pl.when(core != i)
                def _():
                    bytes_of(part, 8, 0, i).wait_send()

    def gather(where, i):
        mine = margin_ref.at[band, parts[i]]
        return send(mine, mine, sems.at[3, 0, i], sems.at[3, 1, i], where)

    def sum_part(i):
        @pl.when(has_plane)
        def _():
            bytes_of(band_in, 11, 0, i).wait_recv()

        @pl.when(jnp.logical_not(has_plane))
        def _():
            bytes_of(band_in, 12, 0, i).wait_recv()

        hi_in[hi, parts[i], :] = total_of(band_in, 12, i)
        for k in FAR_HI:
            across_hi(k, i).start()
        filter_sent()
        bytes_of(hi_in, 3, 1, i).wait_recv()
        z_in[z, parts[i], :] = total_of(hi_in, 4, i)
        for k in FAR_Z:
            across_z(k, i).start()
        bytes_of(hi_in, 3, 1, i).wait_send()
        bytes_of(z_in, 7, 2, i).wait_recv()
        margin_ref[band, parts[i], :] = total_of(z_in, 8, i) * F32(1.0 / CELLS)
        for k, flip, where in to_sixteen:
            @pl.when(bands[k] < PLANES)
            def _():
                gather(where, i).start()
        bytes_of(z_in, 7, 2, i).wait_send()

        @pl.when(jnp.logical_not(has_plane))
        def _():
            bytes_of(margin_ref, 12, 3, i).wait_send()

    for i in range(2):
        @pl.when(core == i)
        def _():
            sum_part(i)

    def await_part(i):
        @pl.when(core == i)
        def _():
            bytes_of(margin_ref, 7, 3, i).wait_recv()

        @pl.when(core != i)
        def _():
            bytes_of(margin_ref, 8, 3, i).wait_recv()

    def to_rows(t, begin=0, count=ORB):
        return send(made.at[pl.ds(t * ORB + begin, count)], out_ref.at[band, pl.ds(begin, count)],
                    row_sems.at[0, t], row_sems.at[1, band], (t, dom))

    def from_plane(p):
        return send(made.at[rows_of(0)], out_ref.at[p],
                    row_sems.at[0, 0], row_sems.at[1, p], (p, dom))

    lane = lax.broadcasted_iota(jnp.int32, (HALF, HALF), 1)
    row = lax.broadcasted_iota(jnp.int32, (HALF, HALF), 0)

    def block(i):
        return jnp.concatenate([margin_ref[q, 16 * i:16 * i + 16, :] for q in range(8)], axis=0)

    def groups_of(at):
        return [work[at, 8 * g:8 * g + 8, :] for g in range(HALF // 8)]

    def hand_out(t, begin=0, count=ORB):
        @pl.when(band != t)
        def _():
            to_rows(t, begin, count).start()

        @pl.when(band == t)
        def _():
            out_ref[t, begin:begin + count, :] = made[t * ORB + begin:t * ORB + begin + count, :]

    def multiply(groups, begin, end):
        rows = jnp.concatenate(groups[begin // 8:end // 8], axis=0)
        rows = jnp.where(row[begin:end] >= lane[begin:end], rows, 0.0)
        made[HALF + begin:HALF + end, :] = product(rows, cells_ref[HALF:, :])

    def after_rows(n, groups):
        if n == 32:
            for t in range(4):
                hand_out(t)
            cells_ref[HALF:, :] = cells_ref[HALF:, :] - product(below_ref[...], made[:HALF, :])
        elif n == 64:
            multiply(groups, 0, 64)
        elif n == 96:
            hand_out(4)
            hand_out(5)
            multiply(groups, 64, 96)
        elif n == 112:
            hand_out(6)
            multiply(groups, 96, 112)
        elif n == 128:
            hand_out(7, 0, 16)
            multiply(groups, 112, 128)
            hand_out(7, 16, 16)

    @pl.when(has_plane)
    def _():
        await_part(0)
        work[0] = block(0)
        first = jnp.concatenate(eliminate(groups_of(0), HALF), axis=0)
        first = jnp.where(row >= lane, first, 0.0)
        await_part(1)
        below = product(block(1), first, ((1,), (1,)))
        below_ref[...] = below
        work[1] = block(2) - product(below, below, ((1,), (1,)))
        made[:HALF, :] = product(first, cells_ref[:HALF, :])
        eliminate(groups_of(1), HALF, after_rows)
        for i in range(2):
            @pl.when(core == i)
            def _():
                bytes_of(margin_ref, 11, 3, i).wait_send()

    for p in range(PLANES):
        @pl.when(band != p)
        def _():
            from_plane(p).wait_recv()

    @pl.when(has_plane)
    def _():
        for t in range(8):
            @pl.when(band != t)
            def _():
                to_rows(t).wait_send()


def on_device(orbitals, potential):
    dma = pltpu.SemaphoreType.DMA
    piece = (48, 128)
    in_vmem = pl.BlockSpec(memory_space=pltpu.VMEM)
    planes = pl.pallas_call(
        whole_kernel,
        out_shape=pltpu.VMEM((PLANES, ORB, WIDTH), F32),
        in_specs=[pl.BlockSpec(memory_space=pltpu.HBM)] * 3,
        out_specs=in_vmem,
        scratch_shapes=[
            pltpu.VMEM((PLANES, WIDTH), F32),
            pltpu.VMEM((WIDTH, WIDTH), F32),
            pltpu.VMEM((BANDS, WIDTH), F32),
            pltpu.VMEM((2 * PLANES,) + piece, F32),
            pltpu.VMEM((BANDS, WIDTH), F32),
            pltpu.VMEM((2, HALF, HALF), F32),
            pltpu.VMEM((HALF, HALF), F32),
            pltpu.VMEM((4, 3 * PLANES, ORB, WIDTH), F32),
            pltpu.VMEM((CHUNKS, PLANES, CORB, WIDTH), F32),
            pltpu.VMEM((8,) + piece, F32),
            pltpu.VMEM((2 * PLANES,) + piece, F32),
            pltpu.VMEM((4,) + piece, F32),
            pltpu.VMEM((8,) + piece, F32),
            dma((3, CHUNKS, 2)),
            dma((3, CHUNKS, 2)),
            dma((2,)),
            dma((3,)),
            dma((4, 2, 2)),
            dma((2, 8)),
        ],
        compiler_params=pltpu.CompilerParams(
            collective_id=0, has_side_effects=True, vmem_limit_bytes=54 * 1024 * 1024
        ),
        name="filter_orthonormalize",
    )(jnp.transpose(orbitals, (1, 0, 2)), potential, jnp.asarray(plane_matrix()))
    return jnp.transpose(planes, (1, 0, 2))


def solution(mesh):
    placed = (P("band", "dom", None), P("dom", None))
    return jax.shard_map(
        on_device, mesh=mesh, in_specs=placed, out_specs=P("band", "dom", None), check_vma=False
    )
```

```python
import jax
import jax.numpy as jnp
import numpy as np
from jax import lax
from jax.experimental import pallas as pl
from jax.experimental.pallas import tpu as pltpu
from jax.sharding import PartitionSpec as P

NX = 16
ORB = 32
BANDS = 256
PLANES = 6
WIDTH = 256
CELLS = 98304
GROUPS = 8
CHUNKS = 4
CORB = ORB // CHUNKS
PIVOTS = 4
HALF = BANDS // 2

weights = (
    -5369.0 / 1800.0,
    12.0 / 7.0,
    -15.0 / 56.0,
    10.0 / 189.0,
    -1.0 / 112.0,
    2.0 / 1925.0,
    -1.0 / 16632.0,
)
centre = 6.0
half_width = 5.0
along_z = [-0.5 * w / half_width for w in weights]

FAR_BAND = (2, 6, 3, 5, 1, 7, 4)
FAR_HI = (2, 1, 3)
FAR_Z = (4, 3, 5, 2, 6, 1, 7)
MESH = pl.DeviceIdType.MESH
EXACT = lax.Precision.HIGHEST
F32 = jnp.float32


def plane_matrix():
    out = np.zeros((WIDTH, WIDTH))
    for cell in range(WIDTH):
        y, x = divmod(cell, NX)
        out[cell, cell] += 3.0 * weights[0]
        for step in range(1, 7):
            for sign in (-1, 1):
                out[(y + sign * step) % NX * NX + x, cell] += weights[step]
                out[y * NX + (x + sign * step) % NX, cell] += weights[step]
    return (-0.5 / half_width * out).astype(np.float32)


def product(a, b, dims=((1,), (0,))):
    return lax.dot_general(
        a, b, (dims, ((), ())), precision=EXACT, preferred_element_type=F32
    )


def greet(partners):
    barrier = pltpu.get_barrier_semaphore()
    for partner in partners:
        pl.semaphore_signal(barrier, inc=1, device_id=partner, device_id_type=MESH)
    pl.semaphore_wait(barrier, len(partners))


def send(src, dst, send_sem, recv_sem, device):
    copy = pltpu.make_async_remote_copy(
        src_ref=src,
        dst_ref=dst,
        send_sem=send_sem,
        recv_sem=recv_sem,
        device_id=device,
        device_id_type=MESH,
    )
    return copy


def eliminate(groups, size, after_rows=None):
    lane = lax.broadcasted_iota(jnp.int32, (8, size), 1)
    sublane = lax.broadcasted_iota(jnp.int32, (8, size), 0)
    groups = list(groups)
    span = range(PIVOTS)

    def spread_lane(tile, at):
        return jnp.broadcast_to(tile[:, at:at + 1], (8, size))

    def spread_row(tile, at):
        return jnp.broadcast_to(tile[at:at + 1, :], (8, size))

    entry = None
    for first in range(0, size, PIVOTS):
        home, off = divmod(first, 8)
        live = range(home, size // 8)
        columns = [{g: spread_lane(groups[g], first + q) for g in live} for q in span]
        if entry is None:
            entry = [[spread_row(columns[q][home], off + p) for q in range(p + 1)] for p in span]
        following = first + PIVOTS
        if following < size:
            near, near_off = divmod(following, 8)
            ahead = [spread_lane(groups[near], following + q) for q in span]
            ahead = [[spread_row(ahead[q], near_off + p) for q in range(p + 1)] for p in span]
            coupling = [[spread_row(columns[t][near], near_off + p) for t in span] for p in span]
        inside = (lane >= first) & (lane < following)
        scales = []
        low = [[None] * PIVOTS for _ in span]
        for q in span:
            value = entry[q][q]
            for t in range(q):
                value = value - low[q][t] * low[q][t]
            scales.append(lax.rsqrt(value))
            for p in range(q + 1, PIVOTS):
                value = entry[p][q]
                for t in range(q):
                    value = value - low[p][t] * low[q][t]
                low[p][q] = value * scales[q]
        if following < size:
            for t in span:
                for p in span:
                    value = coupling[p][t]
                    for u in range(t):
                        value = value - low[t][u] * coupling[p][u]
                    coupling[p][t] = value * scales[t]
            for p in span:
                for q in range(p + 1):
                    value = ahead[p][q]
                    for t in span:
                        value = value - coupling[p][t] * coupling[q][t]
                    ahead[p][q] = value
            entry = ahead
        scaled = []
        pivot_rows = []
        for q in span:
            column = dict(columns[q])
            row = spread_row(groups[home], off + q)
            row = jnp.where(inside, jnp.where(lane == first + q, 1.0, 0.0), row)
            for t in range(q):
                row = row - low[q][t] * pivot_rows[t]
                for g in live:
                    column[g] = column[g] - low[q][t] * scaled[t][g]
            pivot_rows.append(row * scales[q])
            scaled.append({g: column[g] * scales[q] for g in live})
        for g in live:
            if g == home and following % 8 == 0:
                new = groups[g]
            else:
                new = jnp.where(inside, 0.0, groups[g])
                for q in span:
                    new = new - scaled[q][g] * pivot_rows[q]
                if g == home:
                    new = jnp.where(sublane < off, groups[g], new)
            if g == home:
                for q in span:
                    new = jnp.where(sublane == off + q, pivot_rows[q], new)
            groups[g] = new
        if after_rows is not None:
            after_rows(following, groups)
    return groups


def rows_of(b):
    return pl.ds(pl.multiple_of(b * ORB, ORB), ORB)


def whole_kernel(x_ref, pot_hbm, mat_hbm, out_ref, pot_ref, mat_ref, cells_ref, margin_ref, made, work, below_ref,
                 field, local, part, band_in, hi_in, z_in,
                 halo_send, halo_recv, cell_sems, load_sems, sems, row_sems):
    band = lax.axis_index("band")
    dom = lax.axis_index("dom")
    count = lax.axis_size("dom")
    core = lax.rem(dom, 2)
    hi = lax.rem(lax.div(dom, 2), 4)
    z = lax.div(dom, 8)
    left = (band, lax.rem(dom + count - 1, count))
    right = (band, lax.rem(dom + 1, count))
    bands = [lax.rem(band + k, 8) for k in range(8)]
    senders = [lax.rem(band + 8 - k, 8) for k in range(8)]
    to_band = [(bands[k], dom) for k in range(8)]
    to_hi = [(band, z * 8 + lax.rem(hi + k, 4) * 2 + core) for k in range(4)]
    to_z = [(band, lax.rem(z + k, 8) * 8 + hi * 2 + core) for k in range(8)]
    has_plane = band < PLANES
    loads = [
        pltpu.make_async_copy(x_ref, field.at[0, pl.ds(PLANES, PLANES)], load_sems.at[0]),
        pltpu.make_async_copy(mat_hbm, mat_ref, load_sems.at[1]),
        pltpu.make_async_copy(pot_hbm, pot_ref, load_sems.at[2]),
    ]
    for load in loads:
        load.start()
    to_sixteen = [
        (k, flip, (bands[k], dom + flip * (1 - 2 * core)))
        for k in FAR_BAND + (0,) for flip in range(2) if k + flip > 0
    ]
    own = core * 8 + band
    greet([to_z[k] for k in FAR_Z] + [to_hi[k] for k in FAR_HI] + [left, right]
          + [where for k, _, where in to_sixteen if k > 0])

    def chunk(c):
        return pl.ds(c * CORB, CORB)

    def halo(r, c):
        own = field.at[r, pl.ds(PLANES, PLANES), chunk(c)]
        return (
            send(own, field.at[r, pl.ds(2 * PLANES, PLANES), chunk(c)],
                 halo_send.at[r, c, 0], halo_recv.at[r, c, 0], left),
            send(own, field.at[r, pl.ds(0, PLANES), chunk(c)],
                 halo_send.at[r, c, 1], halo_recv.at[r, c, 1], right),
        )

    def in_plane(r, c):
        own = field[r, PLANES:2 * PLANES, c * CORB:(c + 1) * CORB, :]
        flat = own.reshape(PLANES * CORB, WIDTH)
        side = product(flat, mat_ref[...]).reshape(PLANES, CORB, WIDTH)
        for p in range(PLANES):
            diag = (pot_ref[p:p + 1, :] - centre) * (1.0 / half_width)
            local[c, p] = side[p] + diag * own[p]

    def rows_in(c):
        return pl.ds(pl.multiple_of(band * ORB, ORB) + c * CORB, CORB)

    def to_plane(k, c):
        return send(field.at[3, PLANES + bands[k], chunk(c)], cells_ref.at[rows_in(c)],
                    cell_sems.at[0], cell_sems.at[1], to_band[k])

    def all_planes():
        others = cells_ref.at[pl.ds(0, BANDS - ORB)]
        return send(others, others, cell_sems.at[0], cell_sems.at[1], to_band[1])

    for load in loads:
        load.wait()
    for c in range(CHUNKS):
        for copy in halo(0, c):
            copy.start()
    for c in range(CHUNKS):
        in_plane(0, c)
    for r in range(3):
        for c in range(CHUNKS):
            rows = slice(c * CORB, (c + 1) * CORB)
            for copy in halo(r, c):
                copy.wait_recv()
            for p in range(PLANES):
                total = local[c, p]
                for step in range(1, 7):
                    total = total + along_z[step] * (
                        field[r, PLANES + p - step, rows, :] + field[r, PLANES + p + step, rows, :]
                    )
                if r > 0:
                    total = 2.0 * total - field[r - 1, PLANES + p, rows, :]
                field[r + 1, PLANES + p, rows, :] = total
            if r < 2:
                for copy in halo(r + 1, c):
                    copy.start()
                in_plane(r + 1, c)
            else:
                for k in FAR_BAND:
                    @pl.when(bands[k] < PLANES)
                    def _():
                        to_plane(k, c).start()

                @pl.when(has_plane)
                def _():
                    cells_ref[rows_in(c), :] = field[3, PLANES + band, rows, :]

    def sixteenth(k, flip):
        return (core + flip * (1 - 2 * core)) * 8 + bands[k]

    parts = (pl.ds(0, 8), pl.ds(8, 16))

    def total_of(ref, count, i):
        total = ref[0, parts[i], :]
        for t in range(1, count):
            total = total + ref[t, parts[i], :]
        return total

    def bytes_of(ref, count, stage, i):
        some = ref.at[pl.ds(0, count), parts[i]]
        return send(some, some, sems.at[stage, 0, i], sems.at[stage, 1, i], left)

    def to_owner(k, flip, where, i):
        return send(part.at[sixteenth(k, flip), parts[i]], band_in.at[core * PLANES + band, parts[i]],
                    sems.at[0, 0, i], sems.at[0, 1, i], where)

    @pl.when(has_plane)
    def _():
        all_planes().wait_recv()
        for i in range(2):
            if i == 0:
                blocks = (product(cells_ref[:HALF, :], cells_ref[:HALF, :], ((1,), (1,))),)
            else:
                both = product(cells_ref[HALF:, :], cells_ref[...], ((1,), (1,)))
                blocks = (both[:, :HALF], both[:, HALF:])
            for q in range(16):
                for n, piece in enumerate(blocks):
                    part[q, 8 * (i + n):8 * (i + n) + 8, :] = piece[8 * q:8 * q + 8, :]
            for target in to_sixteen:
                to_owner(*target, i).start()
            band_in[core * PLANES + band, parts[i], :] = part[own, parts[i], :]

    def across_hi(k, i):
        mine = hi_in.at[hi, parts[i]]
        return send(mine, mine, sems.at[1, 0, i], sems.at[1, 1, i], to_hi[k])

    for i in range(2):
        @pl.when(has_plane)
        def _():
            bytes_of(band_in, 11, 0, i).wait_recv()

        @pl.when(jnp.logical_not(has_plane))
        def _():
            bytes_of(band_in, 12, 0, i).wait_recv()

        hi_in[hi, parts[i], :] = total_of(band_in, 12, i)
        for k in FAR_HI:
            across_hi(k, i).start()

    def across_z(k, i):
        mine = z_in.at[z, parts[i]]
        return send(mine, mine, sems.at[2, 0, i], sems.at[2, 1, i], to_z[k])

    def sent_planes(count):
        out = field.at[3, pl.ds(PLANES, count)]
        return send(out, out, cell_sems.at[0], cell_sems.at[1], left)

    def filter_sent():
        for c in range(CHUNKS):
            for r in range(3):
                for copy in halo(r, c):
                    copy.wait_send()

        @pl.when(jnp.logical_not(has_plane))
        def _():
            sent_planes(PLANES).wait_send()

        @pl.when(has_plane)
        def _():
            sent_planes(PLANES - 1).wait_send()
            for i in range(2):
                bytes_of(part, 15, 0, i).wait_send()

    for i in range(2):
        bytes_of(hi_in, 3, 1, i).wait_recv()
        z_in[z, parts[i], :] = total_of(hi_in, 4, i)
        for k in FAR_Z:
            across_z(k, i).start()
        if i == 0:
            filter_sent()

    def gather(where, i):
        mine = margin_ref.at[own, parts[i]]
        return send(mine, mine, sems.at[3, 0, i], sems.at[3, 1, i], where)

    for i in range(2):
        bytes_of(hi_in, 3, 1, i).wait_send()
        bytes_of(z_in, 7, 2, i).wait_recv()
        margin_ref[own, parts[i], :] = total_of(z_in, 8, i) * F32(1.0 / CELLS)
        for k in FAR_BAND + (0,):
            @pl.when(bands[k] < PLANES)
            def _():
                for other, _, where in to_sixteen:
                    if other == k:
                        gather(where, i).start()

    def to_rows(t, begin=0, count=ORB):
        return send(made.at[pl.ds(t * ORB + begin, count)], out_ref.at[band, pl.ds(begin, count)],
                    row_sems.at[0, t], row_sems.at[1, band], (t, dom))

    def from_plane(p):
        return send(made.at[rows_of(0)], out_ref.at[p],
                    row_sems.at[0, 0], row_sems.at[1, p], (p, dom))

    lane = lax.broadcasted_iota(jnp.int32, (HALF, HALF), 1)
    row = lax.broadcasted_iota(jnp.int32, (HALF, HALF), 0)

    def block(i):
        return jnp.concatenate([margin_ref[q, 8 * i:8 * i + 8, :] for q in range(16)], axis=0)

    def groups_of(at):
        return [work[at, 8 * g:8 * g + 8, :] for g in range(HALF // 8)]

    def hand_out(t, begin=0, count=ORB):
        @pl.when(band != t)
        def _():
            to_rows(t, begin, count).start()

        @pl.when(band == t)
        def _():
            out_ref[t, begin:begin + count, :] = made[t * ORB + begin:t * ORB + begin + count, :]

    def multiply(groups, begin, end):
        rows = jnp.concatenate(groups[begin // 8:end // 8], axis=0)
        rows = jnp.where(row[begin:end] >= lane[begin:end], rows, 0.0)
        made[HALF + begin:HALF + end, :] = product(rows, cells_ref[HALF:, :])

    def after_rows(n, groups):
        if n == 32:
            for t in range(4):
                hand_out(t)
            cells_ref[HALF:, :] = cells_ref[HALF:, :] - product(below_ref[...], made[:HALF, :])
        elif n == 64:
            multiply(groups, 0, 64)
        elif n == 96:
            hand_out(4)
            hand_out(5)
            multiply(groups, 64, 96)
        elif n == 112:
            hand_out(6)
            multiply(groups, 96, 112)
        elif n == 120:
            hand_out(7, 0, 16)
            multiply(groups, 112, 120)
        elif n == 128:
            hand_out(7, 16, 8)
            multiply(groups, 120, 128)
            hand_out(7, 24, 8)

    @pl.when(jnp.logical_not(has_plane))
    def _():
        for i in range(2):
            bytes_of(z_in, 7, 2, i).wait_send()
            bytes_of(margin_ref, 12, 3, i).wait_send()

    @pl.when(has_plane)
    def _():
        bytes_of(margin_ref, 15, 3, 0).wait_recv()
        work[0] = block(0)
        first = jnp.concatenate(eliminate(groups_of(0), HALF), axis=0)
        first = jnp.where(row >= lane, first, 0.0)
        bytes_of(margin_ref, 15, 3, 1).wait_recv()
        below = product(block(1), first, ((1,), (1,)))
        below_ref[...] = below
        work[1] = block(2) - product(below, below, ((1,), (1,)))
        made[:HALF, :] = product(first, cells_ref[:HALF, :])
        eliminate(groups_of(1), HALF, after_rows)
        for i in range(2):
            bytes_of(z_in, 7, 2, i).wait_send()
            bytes_of(margin_ref, 11, 3, i).wait_send()

    for p in range(PLANES):
        @pl.when(band != p)
        def _():
            from_plane(p).wait_recv()

    @pl.when(has_plane)
    def _():
        for t in range(8):
            @pl.when(band != t)
            def _():
                to_rows(t).wait_send()


def on_device(orbitals, potential):
    dma = pltpu.SemaphoreType.DMA
    piece = (24, 128)
    in_vmem = pl.BlockSpec(memory_space=pltpu.VMEM)
    planes = pl.pallas_call(
        whole_kernel,
        out_shape=pltpu.VMEM((PLANES, ORB, WIDTH), F32),
        in_specs=[pl.BlockSpec(memory_space=pltpu.HBM)] * 3,
        out_specs=in_vmem,
        scratch_shapes=[
            pltpu.VMEM((PLANES, WIDTH), F32),
            pltpu.VMEM((WIDTH, WIDTH), F32),
            pltpu.VMEM((BANDS, WIDTH), F32),
            pltpu.VMEM((16,) + piece, F32),
            pltpu.VMEM((BANDS, WIDTH), F32),
            pltpu.VMEM((2, HALF, HALF), F32),
            pltpu.VMEM((HALF, HALF), F32),
            pltpu.VMEM((4, 3 * PLANES, ORB, WIDTH), F32),
            pltpu.VMEM((CHUNKS, PLANES, CORB, WIDTH), F32),
            pltpu.VMEM((16,) + piece, F32),
            pltpu.VMEM((2 * PLANES,) + piece, F32),
            pltpu.VMEM((4,) + piece, F32),
            pltpu.VMEM((8,) + piece, F32),
            dma((3, CHUNKS, 2)),
            dma((3, CHUNKS, 2)),
            dma((2,)),
            dma((3,)),
            dma((4, 2, 2)),
            dma((2, 8)),
        ],
        compiler_params=pltpu.CompilerParams(
            collective_id=0, has_side_effects=True, vmem_limit_bytes=54 * 1024 * 1024
        ),
        name="filter_orthonormalize",
    )(jnp.transpose(orbitals, (1, 0, 2)), potential, jnp.asarray(plane_matrix()))
    return jnp.transpose(planes, (1, 0, 2))


def solution(mesh):
    placed = (P("band", "dom", None), P("dom", None))
    return jax.shard_map(
        on_device, mesh=mesh, in_specs=placed, out_specs=P("band", "dom", None), check_vma=False
    )
```
